512 devices in a mesh: dp: 64 (over x, y, z_hi), tensor: 8 (over z_lo, core).
Axes of the slice: x: 4, y: 8, z: 8 (z_hi: 2, z_lo: 4; z = z_hi * 4 + z_lo), core: 2. Of those that a mesh axis runs over, the one named last changes fastest.
Arguments:
- layer_input: bfloat16 [8192, 8192], P('dp', 'tensor'), may hold values from -60 to 60
- residual_grad: bfloat16 [8192, 8192], P('dp', 'tensor'), may hold values from -4 to 4
- key_value_grad: bfloat16 [8192, 1024], P('dp', 'tensor'), may hold values from -12 to 12
- kv_weight: bfloat16 [1024, 8192], P('tensor', 'dp'), may hold values from -0.0625 to 0.0625
- norm_gain: float32 [8192], P('tensor'), may hold values from 0.1 to 1.9
Outputs:
- input_grad: bfloat16 [8192, 8192], P('dp', 'tensor')
- weight_grad: float32 [1024, 8192], P('tensor', 'dp')
- gain_grad: float32 [8192], P('tensor')
The draws below stay inside these ranges and needn't reach their ends.
All inputs are finite; a program needn't handle non-finite values.
Results may differ from the reference program's by a relative error of at most 0.0039.
Values may be sent and summed in bfloat16 or wider, within the bound.
No kernel may reach another device: no remote copies, remote signals or barrier semaphores. Data moves between devices by JAX's collectives and lax.ppermute only.
A program may use at most 64 MiB of HBM per device.

```python
import jax
import jax.numpy as jnp
from jax import lax

D = 8192
HD = 128
KVH = 4
TOK_DEV = 128
COLS = 1024
TOKENS = 8192
N_DP = 64
N_TENSOR = 8


def draw_layer_input(key, part):
    key = jax.random.fold_in(key, 11)
    position = jnp.arange(D, dtype=jnp.float32) / (D - 1)
    base = jnp.clip(jax.random.normal(key, (TOKENS, D), jnp.float32), -6.0, 6.0)
    rising = 3.0 ** position
    return (base * rising[None, :]).astype(jnp.bfloat16)


def levels(rng, extent, shards, smallest, top_value):
    gain = 1.0
    for dim, shards_of in shards:
        heights = jax.random.uniform(jax.random.fold_in(jax.random.fold_in(rng, 6), dim), (shards_of,), jnp.float32, smallest / len(shards), top_value / len(shards))
        gain = gain * jnp.repeat(jnp.exp(heights), extent[dim] // shards_of).reshape((-1,) + (1,) * (len(extent) - 1 - dim))
    return gain


def centred(own_key, dims, deviation, limit, pieces=(), kind=jnp.bfloat16):
    entries = deviation * jax.random.normal(own_key, dims, jnp.float32)
    if pieces:
        entries = entries * levels(own_key, dims, pieces, -0.22, 0.18)
    return jnp.clip(entries, -limit, limit).astype(kind)


def setup_inputs(seed: int = 0) -> dict:
    streams_of = jax.random.split(jax.random.key(seed), 6)
    return {
        "layer_input": draw_layer_input(jax.random.fold_in(streams_of[5], 71), 0),
        "residual_grad": centred(streams_of[1], (TOKENS, D), 0.5, 4.0, ((0, 64), (1, 8))),
        "key_value_grad": centred(streams_of[2], (TOKENS, COLS), 2.0, 12.0, ((0, 64), (1, 8))),
        "kv_weight": centred(streams_of[3], (COLS, D), D ** -0.5, 0.0625, ((0, 8), (1, 64))),
        "norm_gain": jnp.clip(1.0 + 0.18 * jax.random.normal(streams_of[4], (D,), jnp.float32), 0.1, 1.9),
    }


rope_theta = 500000.0
norm_eps = 1e-05

def rope_tables(positions_count, head_size):
    half_head = head_size // 2
    frequency = rope_theta ** (-(jnp.arange(half_head, dtype=jnp.float32) * 2.0 / head_size))
    angles = jnp.arange(positions_count, dtype=jnp.float32)[:, None] * frequency[None, :]
    return (jnp.cos(angles), jnp.sin(angles))

def unrotate(grads, cosine, sine):
    half_head = grads.shape[-1] // 2
    lower_part = grads[..., :half_head]
    upper_part = grads[..., half_head:]
    return jnp.concatenate([lower_part * cosine + upper_part * sine, upper_part * cosine - lower_part * sine], axis=-1)

def reference(layer_input, residual_grad, key_value_grad, kv_weight, norm_gain):
    row_total = layer_input.shape[0]
    cosine, sine = rope_tables(TOK_DEV, HD)
    cosine = jnp.tile(cosine, (N_DP, 1))[:, None, :]
    sine = jnp.tile(sine, (N_DP, 1))[:, None, :]
    blocks = key_value_grad.astype(jnp.float32).reshape(row_total, 2 * KVH, HD)
    turned = unrotate(blocks, cosine, sine)
    is_key = (jnp.arange(2 * KVH) % 2 == 0)[None, :, None]
    kv_pre = jnp.where(is_key, turned, blocks).reshape(row_total, 2 * KVH * HD).astype(jnp.bfloat16)
    widened = layer_input.astype(jnp.float32)
    inv_scale = lax.rsqrt(lax.optimization_barrier(jnp.mean(widened * widened, axis=1, keepdims=True)) + norm_eps)
    normal = widened * inv_scale
    normed = (normal * norm_gain[None, :]).astype(jnp.bfloat16)
    group_cols = 2 * KVH * HD // N_TENSOR
    norm_grad = jnp.zeros((row_total, D), jnp.float32)
    for member in range(N_TENSOR):
        product = jnp.dot(kv_pre[:, member * group_cols:(member + 1) * group_cols], kv_weight[member * group_cols:(member + 1) * group_cols, :], preferred_element_type=jnp.float32).astype(jnp.bfloat16)
        product = lax.optimization_barrier(product)
        norm_grad = norm_grad + product.astype(jnp.float32)
    scaled = norm_gain[None, :] * norm_grad
    inner = lax.optimization_barrier(jnp.mean(scaled * normal, axis=1, keepdims=True))
    input_grad = (residual_grad.astype(jnp.float32) + inv_scale * (scaled - normal * inner)).astype(jnp.bfloat16)
    weight_grad = jnp.dot(kv_pre.T, normed, preferred_element_type=jnp.float32)
    gain_grad = lax.optimization_barrier(jnp.sum(norm_grad * normal, axis=0))
    return (input_grad, weight_grad, gain_grad)
```

```python
import jax
import jax.numpy as jnp
from jax import lax
from jax.sharding import Mesh
from jax.sharding import PartitionSpec as P

D = 8192
HD = 128
TOK = 128

rope_theta = 500000.0
norm_eps = 1e-05

SIZES = (4, 8, 2, 4, 2)
AXES = ("x", "y", "zh", "zl", "core")
DP = ("x", "y", "zh")
TENSOR = ("zl", "core")
ROW = ("y", "zh")


def flat_index(x, y, zh, zl, core):
    return (((x * 8 + y) * 2 + zh) * 4 + zl) * 2 + core


def weight_moves():
    moves = []
    for x in range(4):
        for y in range(8):
            for zh in range(2):
                for zl in range(4):
                    for core in range(2):
                        there = flat_index(y % 4, zl * 2 + core, zh, x, y // 4)
                        moves.append((flat_index(x, y, zh, zl, core), there))
    return moves


def exchange(value, axes):
    return lax.all_to_all(value, axes, split_axis=0, concat_axis=0, tiled=True)


def spread(value, axes, count):
    return exchange(jnp.broadcast_to(value[None], (count,) + value.shape), axes)


def rope_tables(positions_count, head_size):
    half_head = head_size // 2
    frequency = rope_theta ** (-(jnp.arange(half_head, dtype=jnp.float32) * 2.0 / head_size))
    angles = jnp.arange(positions_count, dtype=jnp.float32)[:, None] * frequency[None, :]
    return (jnp.cos(angles), jnp.sin(angles))


def shards(layer_input, residual_grad, key_value_grad, kv_weight, norm_gain):
    moves = weight_moves()
    quarter = layer_input.shape[1] // 4

    cut = layer_input.reshape(TOK, 4, quarter).transpose(1, 0, 2)
    rows = exchange(cut, "x").reshape(4 * TOK, quarter)

    moved = lax.ppermute(kv_weight, AXES, moves)
    weights = spread(moved, ROW, 16).reshape(8, 2, HD, HD)

    cosine, sine = rope_tables(TOK, HD)
    grads = key_value_grad.astype(jnp.float32)
    low, high = grads[:, : HD // 2], grads[:, HD // 2 :]
    turned = jnp.concatenate([low * cosine + high * sine, high * cosine - low * sine], axis=1)
    is_key = lax.axis_index("core") == 0
    kv_pre = jnp.where(is_key, turned, grads).astype(jnp.bfloat16)

    widened = layer_input.astype(jnp.float32)
    squares = jnp.sum(widened * widened, axis=1)
    first = lax.reduce_precision(squares, 8, 7)
    second = lax.reduce_precision(squares - first, 8, 7)
    third = squares - first - second
    terms = jnp.stack([first, second, third]).astype(jnp.bfloat16)
    terms = jnp.pad(terms, ((0, 13), (0, 0)))
    packet = jnp.concatenate([kv_pre, terms], axis=0)

    packets = spread(packet, "zl", 4)
    packets = spread(packets, "x", 4)
    packets = spread(packets, "core", 2)
    packets = packets.reshape(2, 4, 4, TOK + 16, HD)
    kv = packets[:, :, :, :TOK].transpose(2, 0, 1, 3, 4).reshape(8, 4 * TOK, HD)
    total = jnp.sum(packets[:, :, :, TOK : TOK + 3].astype(jnp.float32), axis=(0, 2, 3))
    inv_all = lax.rsqrt(total / D + norm_eps)
    inv_rows = inv_all.reshape(4 * TOK, 1)
    mine = lax.axis_index("x")
    inv_scale = lax.dynamic_index_in_dim(inv_all, mine, 0, keepdims=False)[:, None]
    gain_quarter = lax.dynamic_slice_in_dim(norm_gain, mine * quarter, quarter)

    normal = rows.astype(jnp.float32) * inv_rows
    normed = (normal * gain_quarter[None, :]).astype(jnp.bfloat16)

    pieces = jnp.einsum(
        "ktc,tbf->kbcf",
        kv,
        normed.reshape(4 * TOK, 2, HD),
        preferred_element_type=jnp.float32,
    ).astype(jnp.bfloat16)
    arrived = exchange(pieces.reshape(16, HD, HD), ROW)
    block = jnp.sum(arrived.astype(jnp.float32), axis=0)
    weight_grad = lax.ppermute(block, AXES, [(b, a) for a, b in moves])

    products = jnp.einsum(
        "ktc,kbcf->ktbf", kv, weights, preferred_element_type=jnp.float32
    ).astype(jnp.bfloat16)
    norm_grad = jnp.sum(products.astype(jnp.float32), axis=0).reshape(4 * TOK, quarter)
    back = exchange(norm_grad.reshape(4, TOK, quarter), "x")
    scaled_rows = norm_grad * gain_quarter[None, :]
    inner_part = jnp.sum(scaled_rows * normal, axis=1).reshape(4, 1, TOK)
    inner_parts = exchange(
        jnp.broadcast_to(inner_part, (4, 8, TOK)).reshape(32, TOK), ("x",) + TENSOR
    )
    inner = jnp.sum(inner_parts, axis=0)[:, None] / D

    gain_part = jnp.sum(norm_grad * normal, axis=0)
    gain_parts = spread(gain_part, DP, 64)
    gain_grad = jnp.sum(gain_parts.reshape(4, 16, quarter), axis=1).reshape(4 * quarter)

    scaled = back.transpose(1, 0, 2).reshape(TOK, 4 * quarter) * norm_gain[None, :]
    input_grad = (
        residual_grad.astype(jnp.float32)
        + inv_scale * (scaled - widened * inv_scale * inner)
    ).astype(jnp.bfloat16)
    return (input_grad, weight_grad, gain_grad)


def solution(mesh):
    fine = Mesh(mesh.devices.reshape(SIZES), AXES)
    return jax.shard_map(
        shards,
        mesh=fine,
        in_specs=(
            P(DP, TENSOR),
            P(DP, TENSOR),
            P(DP, TENSOR),
            P(TENSOR, DP),
            P(TENSOR),
        ),
        out_specs=(P(DP, TENSOR), P(TENSOR, DP), P(TENSOR)),
        check_vma=False,
    )
```

```python
import jax
import jax.numpy as jnp
from jax import lax
from jax.sharding import Mesh
from jax.sharding import PartitionSpec as P

D = 8192
HD = 128
TOK = 128
QUARTER = 256

rope_theta = 500000.0
norm_eps = 1e-05

SIZES = (4, 8, 2, 4, 2)
AXES = ("x", "y", "zh", "zl", "core")
DP = ("x", "y", "zh")
TENSOR = ("zl", "core")
ROW = ("y", "zh")


def flat_index(x, y, zh, zl, core):
    return (((x * 8 + y) * 2 + zh) * 4 + zl) * 2 + core


def weight_moves():
    moves = []
    for x in range(4):
        for y in range(8):
            for zh in range(2):
                for zl in range(4):
                    for core in range(2):
                        far_zl, far_core = x, y // 4
                        place = ((far_zl - zl) % 4) * 2 + (far_core ^ core)
                        there = flat_index(y % 4, place, zh, far_zl, far_core)
                        moves.append((flat_index(x, y, zh, zl, core), there))
    return moves


def exchange(value, axes):
    return lax.all_to_all(value, axes, split_axis=0, concat_axis=0, tiled=True)


def shift(value, axis, count, step):
    return lax.ppermute(value, axis, [(i, (i + step) % count) for i in range(count)])


def gather(value, axis, count):
    return jnp.stack([value] + [shift(value, axis, count, r) for r in range(1, count)])


def terms_of(value):
    first = lax.reduce_precision(value, 8, 7)
    second = lax.reduce_precision(value - first, 8, 7)
    third = value - first - second
    return jnp.stack([first, second, third]).astype(jnp.bfloat16)


def rope_tables(positions_count, head_size):
    half_head = head_size // 2
    frequency = rope_theta ** (-(jnp.arange(half_head, dtype=jnp.float32) * 2.0 / head_size))
    angles = jnp.arange(positions_count, dtype=jnp.float32)[:, None] * frequency[None, :]
    return (jnp.cos(angles), jnp.sin(angles))


def shards(layer_input, residual_grad, key_value_grad, kv_weight, norm_gain):
    moves = weight_moves()
    mine = lax.axis_index("x")

    moved = lax.ppermute(kv_weight, AXES, moves)

    cosine, sine = rope_tables(TOK, HD)
    grads = key_value_grad.astype(jnp.float32)
    low, high = grads[:, : HD // 2], grads[:, HD // 2 :]
    turned = jnp.concatenate([low * cosine + high * sine, high * cosine - low * sine], axis=1)
    kv_pre = jnp.where(lax.axis_index("core") == 0, turned, grads).astype(jnp.bfloat16)
    widened = layer_input.astype(jnp.float32)
    squares = terms_of(jnp.sum(widened * widened, axis=1))
    packet = jnp.concatenate([kv_pre, jnp.pad(squares, ((0, 13), (0, 0)))], axis=0)

    packets = gather(packet, "zl", 4)
    pieces_x = [
        lax.dynamic_slice_in_dim(layer_input, ((mine + r) % 4) * QUARTER, QUARTER, axis=1)
        for r in range(4)
    ]
    rows = jnp.concatenate([pieces_x[0]] + [shift(pieces_x[r], "x", 4, r) for r in range(1, 4)])
    packets, moved = lax.optimization_barrier((packets, moved))
    weights = exchange(jnp.broadcast_to(moved[None], (16, HD, HD)), ROW).reshape(4, 2, 2, HD, HD)
    packets = gather(packets, "x", 4)
    packets = gather(packets, "core", 2)
    kv = packets[:, :, :, :TOK].transpose(2, 0, 1, 3, 4).reshape(4, 2, 4 * TOK, HD)
    total = jnp.sum(packets[:, :, :, TOK : TOK + 3].astype(jnp.float32), axis=(0, 2, 3))
    inv_all = lax.rsqrt(total / D + norm_eps)
    inv_scale = inv_all[0][:, None]
    gain_quarter = lax.dynamic_slice_in_dim(norm_gain, mine * QUARTER, QUARTER)
    normal = rows.astype(jnp.float32) * inv_all.reshape(4 * TOK, 1)
    normed = (normal * gain_quarter[None, :]).astype(jnp.bfloat16)

    products = jnp.einsum(
        "zktc,zkbcf->zktbf", kv, weights, preferred_element_type=jnp.float32
    ).astype(jnp.bfloat16)
    norm_grad = jnp.sum(products.astype(jnp.float32), axis=(0, 1)).reshape(4 * TOK, QUARTER)
    gain_part = jnp.sum(norm_grad * normal, axis=0)

    pieces = jnp.einsum(
        "zktc,tbf->zkbcf",
        kv,
        normed.reshape(4 * TOK, 2, HD),
        preferred_element_type=jnp.float32,
    ).astype(jnp.bfloat16).reshape(16, HD, HD)
    gain_terms = jnp.pad(terms_of(gain_part).reshape(6, HD), ((0, 10), (0, 0)))
    gain_terms = jnp.broadcast_to(gain_terms[None], (16, 16, HD))
    arrived = exchange(jnp.concatenate([pieces, gain_terms], axis=1), ROW)
    block = jnp.sum(arrived[:, :HD].astype(jnp.float32), axis=0)
    weight_grad = lax.ppermute(block, AXES, [(b, a) for a, b in moves])
    gain_sum = jnp.sum(arrived[:, HD : HD + 6].astype(jnp.float32), axis=0)
    gain_sum = jnp.sum(gain_sum.reshape(3, 1, QUARTER), axis=0)
    gain_sums = gather(gain_sum, "x", 4).reshape(4, 1, QUARTER)
    place = (mine - jnp.arange(4)) % 4
    chosen = place[None, :, None] == jnp.arange(4)[:, None, None]
    gain_grad = jnp.sum(jnp.where(chosen, gain_sums, 0.0), axis=0).reshape(4 * QUARTER)

    full = jnp.zeros((TOK, 4 * QUARTER), jnp.float32)
    for r in range(4):
        part = norm_grad[r * TOK : (r + 1) * TOK]
        if r:
            part = shift(part, "x", 4, -r)
        full = lax.dynamic_update_slice_in_dim(full, part, ((mine + r) % 4) * QUARTER, axis=1)
    scaled = full * norm_gain[None, :]
    normal = widened * inv_scale
    inner = jnp.sum(scaled * normal, axis=1)
    inner = inner + shift(inner, "core", 2, 1)
    inner_all = gather(inner, "zl", 4)
    inner = jnp.sum(inner_all, axis=0)[:, None] / D
    input_grad = (
        residual_grad.astype(jnp.float32) + inv_scale * (scaled - normal * inner)
    ).astype(jnp.bfloat16)
    return (input_grad, weight_grad, gain_grad)


def solution(mesh):
    fine = Mesh(mesh.devices.reshape(SIZES), AXES)
    return jax.shard_map(
        shards,
        mesh=fine,
        in_specs=(
            P(DP, TENSOR),
            P(DP, TENSOR),
            P(DP, TENSOR),
            P(TENSOR, DP),
            P(TENSOR),
        ),
        out_specs=(P(DP, TENSOR), P(TENSOR, DP), P(TENSOR)),
        check_vma=False,
    )
```

```python
import jax
import jax.numpy as jnp
from jax import lax
from jax.sharding import Mesh
from jax.sharding import PartitionSpec as P

D = 8192
HD = 128
TOK = 128
QUARTER = 256

rope_theta = 500000.0
norm_eps = 1e-05

SIZES = (4, 8, 2, 4, 2)
AXES = ("x", "y", "zh", "zl", "core")
DP = ("x", "y", "zh")
TENSOR = ("zl", "core")
ROW = ("y", "zh")


def flat_index(x, y, zh, zl, core):
    return (((x * 8 + y) * 2 + zh) * 4 + zl) * 2 + core


def weight_moves():
    moves = []
    for x in range(4):
        for y in range(8):
            for zh in range(2):
                for zl in range(4):
                    for core in range(2):
                        far_zl, far_core = x, y // 4
                        place = (far_zl ^ zl) * 2 + (far_core ^ core)
                        there = flat_index(y % 4, place, zh, far_zl, far_core)
                        moves.append((flat_index(x, y, zh, zl, core), there))
    return moves


def exchange(value, axes):
    return lax.all_to_all(value, axes, split_axis=0, concat_axis=0, tiled=True)


def swap(value, axis, mask):
    count = lax.axis_size(axis)
    return lax.ppermute(value, axis, [(i, i ^ mask) for i in range(count)])


def terms_of(value):
    first = lax.reduce_precision(value, 8, 7)
    second = lax.reduce_precision(value - first, 8, 7)
    third = value - first - second
    return jnp.stack([first, second, third]).astype(jnp.bfloat16)


def rope_tables(positions_count, head_size):
    half_head = head_size // 2
    frequency = rope_theta ** (-(jnp.arange(half_head, dtype=jnp.float32) * 2.0 / head_size))
    angles = jnp.arange(positions_count, dtype=jnp.float32)[:, None] * frequency[None, :]
    return (jnp.cos(angles), jnp.sin(angles))


def shards(layer_input, residual_grad, key_value_grad, kv_weight, norm_gain):
    moves = weight_moves()
    mine = lax.axis_index("x")

    def quarter(value, r):
        return lax.dynamic_slice_in_dim(value, (mine ^ r) * QUARTER, QUARTER, axis=value.ndim - 1)

    moved = lax.ppermute(kv_weight, AXES, moves)

    near = swap(jnp.concatenate([quarter(layer_input, 3), quarter(layer_input, 2)]), "x", 3)
    own = quarter(layer_input, 0)
    far = swap(jnp.concatenate([quarter(layer_input, 1), near[TOK:]]), "x", 1)
    rows = jnp.concatenate([own, far[:TOK], near[:TOK], far[TOK:]])

    cosine, sine = rope_tables(TOK, HD)
    grads = key_value_grad.astype(jnp.float32)
    low, high = grads[:, : HD // 2], grads[:, HD // 2 :]
    turned = jnp.concatenate([low * cosine + high * sine, high * cosine - low * sine], axis=1)
    kv_pre = jnp.where(lax.axis_index("core") == 0, turned, grads).astype(jnp.bfloat16)
    widened = layer_input.astype(jnp.float32)
    squares = terms_of(jnp.sum(widened * widened, axis=1))
    packet = jnp.concatenate([kv_pre, jnp.pad(squares, ((0, 13), (0, 0)))], axis=0)[None]

    for mask in (1, 2):
        packet = jnp.concatenate([packet, swap(packet, "zl", mask)])
    packet, moved = lax.optimization_barrier((packet, moved))
    weights = exchange(jnp.broadcast_to(moved[None], (16, HD, HD)), ROW)
    packet = packet[None]
    for mask in (1, 3):
        packet = jnp.concatenate([packet, swap(packet, "x", mask)])
    packet, weights = lax.optimization_barrier((packet, weights))
    weights = weights.reshape(4, 2, 2, HD, HD)
    packet = jnp.stack([packet, swap(packet, "core", 1)])

    kv = packet[:, :, :, :TOK].transpose(2, 0, 1, 3, 4).reshape(4, 2, 4 * TOK, HD)
    total = jnp.sum(packet[:, :, :, TOK : TOK + 3].astype(jnp.float32), axis=(0, 2, 3))
    inv_all = lax.rsqrt(total / D + norm_eps)
    inv_scale = inv_all[0][:, None]
    gain_quarter = quarter(norm_gain, 0)
    normal = rows.astype(jnp.float32) * inv_all.reshape(4 * TOK, 1)
    normed = (normal * gain_quarter[None, :]).astype(jnp.bfloat16)

    products = jnp.einsum(
        "zktc,zkbcf->zktbf", kv, weights, preferred_element_type=jnp.float32
    ).astype(jnp.bfloat16)
    norm_grad = jnp.sum(products.astype(jnp.float32), axis=(0, 1)).reshape(4 * TOK, QUARTER)
    gain_part = jnp.sum(norm_grad * normal, axis=0)

    sent = norm_grad.astype(jnp.bfloat16)
    near = swap(sent[2 * TOK :], "x", 3)
    far = swap(jnp.concatenate([sent[TOK : 2 * TOK], near[TOK:]]), "x", 1)

    pieces = jnp.einsum(
        "zktc,tbf->zkbcf",
        kv,
        normed.reshape(4 * TOK, 2, HD),
        preferred_element_type=jnp.float32,
    ).astype(jnp.bfloat16).reshape(16, HD, HD)
    gain_terms = jnp.pad(terms_of(gain_part).reshape(6, HD), ((0, 10), (0, 0)))
    gain_terms = jnp.broadcast_to(gain_terms[None], (16, 16, HD))
    arrived = exchange(jnp.concatenate([pieces, gain_terms], axis=1), ROW)
    block = jnp.sum(arrived[:, :HD].astype(jnp.float32), axis=0)
    weight_grad = lax.ppermute(block, AXES, [(b, a) for a, b in moves])
    gain_sum = jnp.sum(arrived[:, HD : HD + 6].astype(jnp.float32), axis=0)
    gain_sum = jnp.sum(gain_sum.reshape(3, 1, QUARTER), axis=0)
    gain_sum, block = lax.optimization_barrier((gain_sum, block))
    for mask in (1, 3):
        gain_sum = jnp.concatenate([gain_sum, swap(gain_sum, "x", mask)])
    place = mine ^ jnp.array([0, 1, 3, 2])
    chosen = place[None, :, None] == jnp.arange(4)[:, None, None]
    gain_grad = jnp.sum(jnp.where(chosen, gain_sum[None], 0.0), axis=1).reshape(4 * QUARTER)

    full = jnp.zeros((TOK, 4 * QUARTER), jnp.bfloat16)
    for part, r in ((sent[:TOK], 0), (far[:TOK], 1), (near[:TOK], 3), (far[TOK:], 2)):
        full = lax.dynamic_update_slice_in_dim(full, part, (mine ^ r) * QUARTER, axis=1)
    scaled = full.astype(jnp.float32) * norm_gain[None, :]
    normal = widened * inv_scale
    inner = jnp.sum(scaled * normal, axis=1)
    for axis, mask in (("core", 1), ("zl", 1), ("zl", 2)):
        inner = inner + swap(inner, axis, mask)
    inner = inner[:, None] / D
    input_grad = (
        residual_grad.astype(jnp.float32) + inv_scale * (scaled - normal * inner)
    ).astype(jnp.bfloat16)
    return (input_grad, weight_grad, gain_grad)


def solution(mesh):
    fine = Mesh(mesh.devices.reshape(SIZES), AXES)
    return jax.shard_map(
        shards,
        mesh=fine,
        in_specs=(
            P(DP, TENSOR),
            P(DP, TENSOR),
            P(DP, TENSOR),
            P(TENSOR, DP),
            P(TENSOR),
        ),
        out_specs=(P(DP, TENSOR), P(TENSOR, DP), P(TENSOR)),
        check_vma=False,
    )
```

```python
import jax
import jax.numpy as jnp
from jax import lax
from jax.sharding import Mesh
from jax.sharding import PartitionSpec as P

D = 8192
HD = 128
TOK = 128
QUARTER = 256

rope_theta = 500000.0
norm_eps = 1e-05

SIZES = (4, 8, 2, 4, 2)
AXES = ("x", "y", "zh", "zl", "core")
DP = ("x", "y", "zh")
TENSOR = ("zl", "core")
ROW = ("y", "zh")


def flat_index(x, y, zh, zl, core):
    return (((x * 8 + y) * 2 + zh) * 4 + zl) * 2 + core


def weight_moves():
    moves = []
    for x in range(4):
        for y in range(8):
            for zh in range(2):
                for zl in range(4):
                    for core in range(2):
                        far_zl, far_core = x, y // 4
                        place = (far_zl ^ zl) * 2 + (far_core ^ core)
                        there = flat_index(y % 4, place, zh, far_zl, far_core)
                        moves.append((flat_index(x, y, zh, zl, core), there))
    return moves


def exchange(value, axes):
    return lax.all_to_all(value, axes, split_axis=0, concat_axis=0, tiled=True)


def swap(value, axis, mask):
    count = lax.axis_size(axis)
    return lax.ppermute(value, axis, [(i, i ^ mask) for i in range(count)])


def terms_of(value):
    first = lax.reduce_precision(value, 8, 7)
    second = lax.reduce_precision(value - first, 8, 7)
    third = value - first - second
    return jnp.stack([first, second, third]).astype(jnp.bfloat16)


def rope_tables(positions_count, head_size):
    half_head = head_size // 2
    frequency = rope_theta ** (-(jnp.arange(half_head, dtype=jnp.float32) * 2.0 / head_size))
    angles = jnp.arange(positions_count, dtype=jnp.float32)[:, None] * frequency[None, :]
    return (jnp.cos(angles), jnp.sin(angles))


def shards(layer_input, residual_grad, key_value_grad, kv_weight, norm_gain):
    moves = weight_moves()
    mine = lax.axis_index("x")

    def quarter(value, r):
        return lax.dynamic_slice_in_dim(value, (mine ^ r) * QUARTER, QUARTER, axis=value.ndim - 1)

    moved = lax.ppermute(kv_weight, AXES, moves)

    near = swap(jnp.concatenate([quarter(layer_input, 3), quarter(layer_input, 2)]), "x", 3)

    cosine, sine = rope_tables(TOK, HD)
    grads = key_value_grad.astype(jnp.float32)
    low, high = grads[:, : HD // 2], grads[:, HD // 2 :]
    turned = jnp.concatenate([low * cosine + high * sine, high * cosine - low * sine], axis=1)
    kv_pre = jnp.where(lax.axis_index("core") == 0, turned, grads).astype(jnp.bfloat16)
    widened = layer_input.astype(jnp.float32)
    squares = terms_of(jnp.sum(widened * widened, axis=1))
    packet = jnp.concatenate([kv_pre, jnp.pad(squares, ((0, 13), (0, 0)))], axis=0)[None]

    packet = jnp.concatenate([packet, swap(packet, "zl", 1)])
    packet, moved, near = lax.optimization_barrier((packet, moved, near))
    weights = exchange(jnp.broadcast_to(moved[None], (16, HD, HD)), ROW)
    far = swap(jnp.concatenate([quarter(layer_input, 1), near[TOK:]]), "x", 1)
    packet = jnp.concatenate([packet, swap(packet, "zl", 2)])
    packet, far = lax.optimization_barrier((packet, far))
    rows = jnp.concatenate([quarter(layer_input, 0), far[:TOK], near[:TOK], far[TOK:]])
    packet = packet[None]
    packet = jnp.concatenate([packet, swap(packet, "x", 1)])
    packet, weights = lax.optimization_barrier((packet, weights))
    packet = jnp.concatenate([packet, swap(packet, "x", 3)])
    weights = weights.reshape(4, 2, 2, HD, HD)
    packet = jnp.stack([packet, swap(packet, "core", 1)])

    kv = packet[:, :, :, :TOK].transpose(2, 0, 1, 3, 4).reshape(4, 2, 4 * TOK, HD)
    total = jnp.sum(packet[:, :, :, TOK : TOK + 3].astype(jnp.float32), axis=(0, 2, 3))
    inv_all = lax.rsqrt(total / D + norm_eps)
    inv_scale = inv_all[0][:, None]
    gain_quarter = quarter(norm_gain, 0)
    normal = rows.astype(jnp.float32) * inv_all.reshape(4 * TOK, 1)
    normed = (normal * gain_quarter[None, :]).astype(jnp.bfloat16)

    products = jnp.einsum(
        "zktc,zkbcf->zktbf", kv, weights, preferred_element_type=jnp.float32
    ).astype(jnp.bfloat16)
    norm_grad = jnp.sum(products.astype(jnp.float32), axis=(0, 1)).reshape(4 * TOK, QUARTER)
    gain_part = jnp.sum(norm_grad * normal, axis=0)

    sent = norm_grad.astype(jnp.bfloat16)
    near = swap(sent[2 * TOK :], "x", 3)

    pieces = jnp.einsum(
        "zktc,tbf->zkbcf",
        kv,
        normed.reshape(4 * TOK, 2, HD),
        preferred_element_type=jnp.float32,
    ).astype(jnp.bfloat16).reshape(16, HD, HD)
    gain_terms = jnp.pad(terms_of(gain_part).reshape(6, HD), ((0, 10), (0, 0)))
    gain_terms = jnp.broadcast_to(gain_terms[None], (16, 16, HD))
    gain_terms, near = lax.optimization_barrier((gain_terms, near))
    far = swap(jnp.concatenate([sent[TOK : 2 * TOK], near[TOK:]]), "x", 1)
    arrived = exchange(jnp.concatenate([pieces, gain_terms], axis=1), ROW)
    block = jnp.sum(arrived[:, :HD].astype(jnp.float32), axis=0)
    weight_grad = lax.ppermute(block, AXES, [(b, a) for a, b in moves])
    gain_sum = jnp.sum(arrived[:, HD : HD + 6].astype(jnp.float32), axis=0)
    gain_sum = jnp.sum(gain_sum.reshape(3, 1, QUARTER), axis=0)
    gain_sum = jnp.concatenate([gain_sum, swap(gain_sum, "x", 1)])
    gain_sum, weight_grad = lax.optimization_barrier((gain_sum, weight_grad))
    gain_sum = jnp.concatenate([gain_sum, swap(gain_sum, "x", 3)])
    place = mine ^ jnp.array([0, 1, 3, 2])
    chosen = place[None, :, None] == jnp.arange(4)[:, None, None]
    gain_grad = jnp.sum(jnp.where(chosen, gain_sum[None], 0.0), axis=1).reshape(4 * QUARTER)

    full = jnp.zeros((TOK, 4 * QUARTER), jnp.bfloat16)
    for part, r in ((sent[:TOK], 0), (far[:TOK], 1), (near[:TOK], 3), (far[TOK:], 2)):
        full = lax.dynamic_update_slice_in_dim(full, part, (mine ^ r) * QUARTER, axis=1)
    scaled = full.astype(jnp.float32) * norm_gain[None, :]
    normal = widened * inv_scale
    inner = jnp.sum(scaled * normal, axis=1)
    for axis, mask in (("core", 1), ("zl", 1), ("zl", 2)):
        inner = inner + swap(inner, axis, mask)
    inner = inner[:, None] / D
    input_grad = (
        residual_grad.astype(jnp.float32) + inv_scale * (scaled - normal * inner)
    ).astype(jnp.bfloat16)
    return (input_grad, weight_grad, gain_grad)


def solution(mesh):
    fine = Mesh(mesh.devices.reshape(SIZES), AXES)
    return jax.shard_map(
        shards,
        mesh=fine,
        in_specs=(
            P(DP, TENSOR),
            P(DP, TENSOR),
            P(DP, TENSOR),
            P(TENSOR, DP),
            P(TENSOR),
        ),
        out_specs=(P(DP, TENSOR), P(TENSOR, DP), P(TENSOR)),
        check_vma=False,
    )
```

```python
import jax
import jax.numpy as jnp
from jax import lax
from jax.sharding import Mesh
from jax.sharding import PartitionSpec as P

D = 8192
HD = 128
TOK = 128
HALF = 512

rope_theta = 500000.0
norm_eps = 1e-05

SIZES = (2, 2, 8, 2, 4, 2)
AXES = ("xh", "xl", "y", "zh", "zl", "core")
DP = ("xh", "xl", "y", "zh")
TENSOR = ("zl", "core")
ROW = ("xh", "y", "zh")


def flat_index(x, y, zh, zl, core):
    return (((x * 8 + y) * 2 + zh) * 4 + zl) * 2 + core


def weight_moves():
    moves = []
    for x in range(4):
        for y in range(8):
            for zh in range(2):
                for zl in range(4):
                    for core in range(2):
                        far_zl, far_core = x, y // 4
                        place = (far_zl ^ zl) * 2 + (far_core ^ core)
                        far_x = (y % 2) * 2 + y // 2 % 2
                        there = flat_index(far_x, place, zh, far_zl, far_core)
                        moves.append((flat_index(x, y, zh, zl, core), there))
    return moves


def exchange(value, axes):
    return lax.all_to_all(value, axes, split_axis=0, concat_axis=0, tiled=True)


def swap(value, axis, mask):
    count = lax.axis_size(axis)
    return lax.ppermute(value, axis, [(i, i ^ mask) for i in range(count)])


def terms_of(value):
    first = lax.reduce_precision(value, 8, 7)
    second = lax.reduce_precision(value - first, 8, 7)
    third = value - first - second
    return jnp.stack([first, second, third]).astype(jnp.bfloat16)


def rope_tables(positions_count, head_size):
    half_head = head_size // 2
    frequency = rope_theta ** (-(jnp.arange(half_head, dtype=jnp.float32) * 2.0 / head_size))
    angles = jnp.arange(positions_count, dtype=jnp.float32)[:, None] * frequency[None, :]
    return (jnp.cos(angles), jnp.sin(angles))


def shards(layer_input, residual_grad, key_value_grad, kv_weight, norm_gain):
    moves = weight_moves()
    low_half = lax.axis_index("xl") == 0

    moved = lax.ppermute(kv_weight, AXES, moves)
    weights = exchange(jnp.broadcast_to(moved[None], (32, HD, HD)), ROW)

    cosine, sine = rope_tables(TOK, HD)
    grads = key_value_grad.astype(jnp.float32)
    low, high = grads[:, : HD // 2], grads[:, HD // 2 :]
    turned = jnp.concatenate([low * cosine + high * sine, high * cosine - low * sine], axis=1)
    kv_pre = jnp.where(lax.axis_index("core") == 0, turned, grads).astype(jnp.bfloat16)
    widened = layer_input.astype(jnp.float32)
    squares = terms_of(jnp.sum(widened * widened, axis=1))
    packet = jnp.concatenate([kv_pre, jnp.pad(squares, ((0, 13), (0, 0)))], axis=0)[None]
    for mask in (1, 2):
        packet = jnp.concatenate([packet, swap(packet, "zl", mask)])

    split = jnp.stack([layer_input[:, i * HD : (i + 1) * HD] for i in range(8)]).reshape(2, 4, TOK, HD)
    kept = jnp.where(low_half, split[0], split[1])
    given = jnp.where(low_half, split[1], split[0])
    sent = jnp.concatenate([packet.reshape(4 * (TOK + 16), HD), given.reshape(4 * TOK, HD)])
    came = swap(sent, "xl", 1)
    rows = jnp.concatenate([kept, came[4 * (TOK + 16) :].reshape(4, TOK, HD)], axis=1)
    packet = jnp.stack([packet, came[: 4 * (TOK + 16)].reshape(4, TOK + 16, HD)])
    packet, weights = lax.optimization_barrier((packet, weights))
    packet = jnp.stack([packet, swap(packet, "core", 1)])

    kv = packet[:, :, :, :TOK].transpose(2, 0, 1, 3, 4).reshape(8, 2 * TOK, HD)
    total = jnp.sum(packet[:, :, :, TOK : TOK + 3].astype(jnp.float32), axis=(0, 2, 3))
    inv_all = lax.rsqrt(total / D + norm_eps)
    inv_scale = inv_all[0][:, None]
    gain_half = jnp.where(low_half, norm_gain[:HALF], norm_gain[HALF:]).reshape(4, 1, HD)
    normal = rows.astype(jnp.float32) * inv_all.reshape(1, 2 * TOK, 1)
    normed = (normal * gain_half).astype(jnp.bfloat16)

    pieces = jnp.einsum(
        "ktc,xbtf->xkbcf",
        kv,
        normed.reshape(2, 2, 2 * TOK, HD),
        preferred_element_type=jnp.float32,
    ).astype(jnp.bfloat16)
    arrived = exchange(pieces.reshape(32, HD, HD), ROW)
    block = jnp.sum(arrived.astype(jnp.float32), axis=0)
    weight_grad = lax.ppermute(block, AXES, [(b, a) for a, b in moves])

    products = jnp.einsum(
        "ktc,xkbcf->kxbtf",
        kv,
        weights.reshape(2, 8, 2, HD, HD),
        preferred_element_type=jnp.float32,
    ).astype(jnp.bfloat16)
    norm_grad = jnp.sum(products.astype(jnp.float32), axis=0).reshape(4, 2 * TOK, HD)
    gain_sum = jnp.sum(norm_grad * normal, axis=1).reshape(HALF)
    for axis, mask in (("y", 1), ("y", 2), ("zh", 1), ("y", 4), ("xh", 1)):
        gain_sum = gain_sum + swap(gain_sum, axis, mask)
    gain_far = swap(gain_sum, "xl", 1)
    gain_grad = jnp.where(
        low_half, jnp.concatenate([gain_sum, gain_far]), jnp.concatenate([gain_far, gain_sum])
    )

    back = norm_grad.astype(jnp.bfloat16)
    here, far = back[:, :TOK], swap(back[:, TOK:], "xl", 1)
    full = jnp.where(low_half, jnp.concatenate([here, far]), jnp.concatenate([far, here]))
    full = full.transpose(1, 0, 2).reshape(TOK, 2 * HALF)
    scaled = full.astype(jnp.float32) * norm_gain[None, :]
    normal = widened * inv_scale
    inner = jnp.sum(scaled * normal, axis=1)
    for axis, mask in (("core", 1), ("zl", 1), ("zl", 2)):
        inner = inner + swap(inner, axis, mask)
    inner = inner[:, None] / D
    input_grad = (
        residual_grad.astype(jnp.float32) + inv_scale * (scaled - normal * inner)
    ).astype(jnp.bfloat16)
    return (input_grad, weight_grad, gain_grad)


def solution(mesh):
    fine = Mesh(mesh.devices.reshape(SIZES), AXES)
    return jax.shard_map(
        shards,
        mesh=fine,
        in_specs=(
            P(DP, TENSOR),
            P(DP, TENSOR),
            P(DP, TENSOR),
            P(TENSOR, DP),
            P(TENSOR),
        ),
        out_specs=(P(DP, TENSOR), P(TENSOR, DP), P(TENSOR)),
        check_vma=False,
    )
```

```python
import jax
import jax.numpy as jnp
from jax import lax
from jax.sharding import Mesh
from jax.sharding import PartitionSpec as P

D = 8192
HD = 128
TOK = 128
QUARTER = 256

rope_theta = 500000.0
norm_eps = 1e-05

SIZES = (4, 8, 2, 4, 2)
AXES = ("x", "y", "zh", "zl", "core")
DP = ("x", "y", "zh")
TENSOR = ("zl", "core")
ROW = ("y", "zh")


def flat_index(x, y, zh, zl, core):
    return (((x * 8 + y) * 2 + zh) * 4 + zl) * 2 + core


def weight_moves():
    moves = []
    for x in range(4):
        for y in range(8):
            for zh in range(2):
                for zl in range(4):
                    for core in range(2):
                        far_zl, far_core = x, y // 4
                        place = (far_zl ^ zl) * 2 + (far_core ^ core)
                        there = flat_index(y % 4, place, zh, far_zl, far_core)
                        moves.append((flat_index(x, y, zh, zl, core), there))
    return moves


def exchange(value, axes):
    return lax.all_to_all(value, axes, split_axis=0, concat_axis=0, tiled=True)


def swap(value, axis, mask):
    count = lax.axis_size(axis)
    return lax.ppermute(value, axis, [(i, i ^ mask) for i in range(count)])


def terms_of(value):
    first = lax.reduce_precision(value, 8, 7)
    second = lax.reduce_precision(value - first, 8, 7)
    third = value - first - second
    return jnp.stack([first, second, third]).astype(jnp.bfloat16)


def rope_tables(positions_count, head_size):
    half_head = head_size // 2
    frequency = rope_theta ** (-(jnp.arange(half_head, dtype=jnp.float32) * 2.0 / head_size))
    angles = jnp.arange(positions_count, dtype=jnp.float32)[:, None] * frequency[None, :]
    return (jnp.cos(angles), jnp.sin(angles))


def shards(layer_input, residual_grad, key_value_grad, kv_weight, norm_gain):
    moves = weight_moves()
    mine = lax.axis_index("x")

    moved = lax.ppermute(kv_weight, AXES, moves)

    cosine, sine = rope_tables(TOK, HD)
    grads = key_value_grad.astype(jnp.float32)
    low, high = grads[:, : HD // 2], grads[:, HD // 2 :]
    turned = jnp.concatenate([low * cosine + high * sine, high * cosine - low * sine], axis=1)
    kv_pre = jnp.where(lax.axis_index("core") == 0, turned, grads).astype(jnp.bfloat16)
    widened = layer_input.astype(jnp.float32)
    squares = terms_of(jnp.sum(widened * widened, axis=1))
    packet = jnp.concatenate([kv_pre, jnp.pad(squares, ((0, 13), (0, 0)))], axis=0)[None]

    blocks = jnp.stack([layer_input[:, i * HD : (i + 1) * HD] for i in range(8)])

    def quarter(r):
        return lax.dynamic_slice_in_dim(blocks, (mine ^ r) * 2, 2, axis=0)

    packet, moved = lax.optimization_barrier((packet, moved))
    packet = jnp.concatenate([packet, swap(packet, "zl", 1)])
    given = jnp.concatenate([quarter(3), quarter(2)]).reshape(4 * TOK, HD)
    near = swap(given, "x", 3)
    packet = jnp.concatenate([packet, swap(packet, "zl", 2)])
    packet, moved, near = lax.optimization_barrier((packet, moved, near))
    weights = exchange(jnp.broadcast_to(moved[None], (16, HD, HD)), ROW)

    near = near.reshape(2, 2, TOK, HD)
    given = jnp.concatenate([quarter(1), near[1]]).reshape(4 * TOK, HD)
    came = swap(jnp.concatenate([packet.reshape(4 * (TOK + 16), HD), given]), "x", 1)
    far = came[4 * (TOK + 16) :].reshape(2, 2, TOK, HD)
    rows = jnp.concatenate([quarter(0), far[0], near[0], far[1]], axis=1)
    packet = jnp.stack([packet, came[: 4 * (TOK + 16)].reshape(4, TOK + 16, HD)])
    packet = jnp.concatenate([packet, swap(packet, "x", 3)])
    packet, weights = lax.optimization_barrier((packet, weights))
    packet = jnp.stack([packet, swap(packet, "core", 1)])

    kv = packet[:, :, :, :TOK].transpose(2, 0, 1, 3, 4).reshape(8, 4 * TOK, HD)
    total = jnp.sum(packet[:, :, :, TOK : TOK + 3].astype(jnp.float32), axis=(0, 2, 3))
    inv_all = lax.rsqrt(total / D + norm_eps)
    inv_scale = inv_all[0][:, None]
    gain_quarter = lax.dynamic_slice_in_dim(norm_gain, mine * QUARTER, QUARTER).reshape(2, 1, HD)
    normal = rows.astype(jnp.float32) * inv_all.reshape(1, 4 * TOK, 1)
    normed = (normal * gain_quarter).astype(jnp.bfloat16)

    pieces = jnp.einsum(
        "ktc,btf->kbcf", kv, normed, preferred_element_type=jnp.float32
    ).astype(jnp.bfloat16)
    arrived = exchange(pieces.reshape(16, HD, HD), ROW)
    block = jnp.sum(arrived.astype(jnp.float32), axis=0)
    weight_grad = lax.ppermute(block, AXES, [(b, a) for a, b in moves])

    products = jnp.einsum(
        "ktc,kbcf->kbtf",
        kv,
        weights.reshape(8, 2, HD, HD),
        preferred_element_type=jnp.float32,
    ).astype(jnp.bfloat16)
    norm_grad = jnp.sum(products.astype(jnp.float32), axis=0)
    gain_part = terms_of(jnp.sum(norm_grad * normal, axis=1)).reshape(6, HD)

    back = norm_grad.astype(jnp.bfloat16)
    given = jnp.concatenate(
        [back[:, 2 * TOK :].reshape(4 * TOK, HD), jnp.pad(gain_part, ((0, 10), (0, 0)))]
    )
    came = swap(given, "x", 3)
    near, gain_near = came[: 4 * TOK].reshape(2, 2 * TOK, HD), came[4 * TOK : 4 * TOK + 6]
    given = jnp.concatenate(
        [
            back[:, TOK : 2 * TOK].reshape(2 * TOK, HD),
            near[:, TOK:].reshape(2 * TOK, HD),
            gain_part,
            gain_near,
            jnp.zeros((4, HD), jnp.bfloat16),
        ]
    )
    came = swap(given, "x", 1)
    far, gain_far = came[: 4 * TOK].reshape(2, 2, TOK, HD), came[4 * TOK : 4 * TOK + 12]
    gains = jnp.concatenate([gain_part, gain_near, gain_far]).astype(jnp.float32)
    gains = jnp.sum(gains.reshape(4, 3, 2, HD), axis=1)
    place = mine ^ jnp.array([0, 3, 1, 2])
    chosen = place[None, :, None, None] == jnp.arange(4)[:, None, None, None]
    gains = jnp.sum(jnp.where(chosen, gains[None], 0.0), axis=1).reshape(8, HD)
    gains, block = lax.optimization_barrier((gains, block))
    gain_parts = exchange(jnp.broadcast_to(gains[None], (16, 8, HD)), ROW)
    gain_grad = jnp.sum(gain_parts, axis=0).reshape(4 * QUARTER)

    full = jnp.zeros((8, TOK, HD), jnp.bfloat16)
    for part, r in ((back[:, :TOK], 0), (far[0], 1), (near[:, :TOK], 3), (far[1], 2)):
        full = lax.dynamic_update_slice_in_dim(full, part, (mine ^ r) * 2, axis=0)
    full = jnp.concatenate([full[i] for i in range(8)], axis=1)
    scaled = full.astype(jnp.float32) * norm_gain[None, :]
    normal = widened * inv_scale
    inner = jnp.sum(scaled * normal, axis=1)
    for axis, mask in (("core", 1), ("zl", 1), ("zl", 2)):
        inner = inner + swap(inner, axis, mask)
    inner = inner[:, None] / D
    input_grad = (
        residual_grad.astype(jnp.float32) + inv_scale * (scaled - normal * inner)
    ).astype(jnp.bfloat16)
    return (input_grad, weight_grad, gain_grad)


def solution(mesh):
    fine = Mesh(mesh.devices.reshape(SIZES), AXES)
    return jax.shard_map(
        shards,
        mesh=fine,
        in_specs=(
            P(DP, TENSOR),
            P(DP, TENSOR),
            P(DP, TENSOR),
            P(TENSOR, DP),
            P(TENSOR),
        ),
        out_specs=(P(DP, TENSOR), P(TENSOR, DP), P(TENSOR)),
        check_vma=False,
    )
```

```python
import jax
import jax.numpy as jnp
from jax import lax
from jax.sharding import Mesh
from jax.sharding import PartitionSpec as P

D = 8192
HD = 128
TOK = 128
QUARTER = 256

rope_theta = 500000.0
norm_eps = 1e-05

SIZES = (4, 8, 2, 4, 2)
AXES = ("x", "y", "zh", "zl", "core")
DP = ("x", "y", "zh")
TENSOR = ("zl", "core")
ROW = ("y", "zh")


def flat_index(x, y, zh, zl, core):
    return (((x * 8 + y) * 2 + zh) * 4 + zl) * 2 + core


def weight_moves():
    moves = []
    for x in range(4):
        for y in range(8):
            for zh in range(2):
                for zl in range(4):
                    for core in range(2):
                        far_zl, far_core = x, y // 4
                        place = (far_zl ^ zl) * 2 + (far_core ^ core)
                        there = flat_index(y % 4, place, zh, far_zl, far_core)
                        moves.append((flat_index(x, y, zh, zl, core), there))
    return moves


def exchange(value, axes):
    return lax.all_to_all(value, axes, split_axis=0, concat_axis=0, tiled=True)


def swap(value, axis, mask):
    count = lax.axis_size(axis)
    return lax.ppermute(value, axis, [(i, i ^ mask) for i in range(count)])


def terms_of(value):
    first = lax.reduce_precision(value, 8, 7)
    second = lax.reduce_precision(value - first, 8, 7)
    third = value - first - second
    return jnp.stack([first, second, third]).astype(jnp.bfloat16)


def rope_tables(positions_count, head_size):
    half_head = head_size // 2
    frequency = rope_theta ** (-(jnp.arange(half_head, dtype=jnp.float32) * 2.0 / head_size))
    angles = jnp.arange(positions_count, dtype=jnp.float32)[:, None] * frequency[None, :]
    return (jnp.cos(angles), jnp.sin(angles))


def shards(layer_input, residual_grad, key_value_grad, kv_weight, norm_gain):
    moves = weight_moves()
    mine = lax.axis_index("x")

    moved = lax.ppermute(kv_weight, AXES, moves)

    cosine, sine = rope_tables(TOK, HD)
    grads = key_value_grad.astype(jnp.float32)
    low, high = grads[:, : HD // 2], grads[:, HD // 2 :]
    turned = jnp.concatenate([low * cosine + high * sine, high * cosine - low * sine], axis=1)
    kv_pre = jnp.where(lax.axis_index("core") == 0, turned, grads).astype(jnp.bfloat16)
    widened = layer_input.astype(jnp.float32)
    squares = terms_of(jnp.sum(widened * widened, axis=1))
    packet = jnp.concatenate([kv_pre, jnp.pad(squares, ((0, 13), (0, 0)))], axis=0)[None]

    blocks = jnp.stack([layer_input[:, i * HD : (i + 1) * HD] for i in range(8)])

    def quarter(r):
        return lax.dynamic_slice_in_dim(blocks, (mine ^ r) * 2, 2, axis=0)

    packet, moved = lax.optimization_barrier((packet, moved))
    other = swap(moved, "zh", 1)
    first = lax.axis_index("zh") == 0
    wide = jnp.stack([jnp.where(first, moved, other), jnp.where(first, other, moved)])
    packet = jnp.concatenate([packet, swap(packet, "zl", 1)])
    packet, wide = lax.optimization_barrier((packet, wide))
    wide = jnp.stack([wide, swap(wide, "core", 1)])
    weights = lax.all_gather(wide, "y", axis=0)[:, 0]
    given = jnp.concatenate([quarter(3), quarter(2)]).reshape(4 * TOK, HD)
    near = swap(given, "x", 3)
    packet = jnp.concatenate([packet, swap(packet, "zl", 2)])
    packet, near = lax.optimization_barrier((packet, near))

    near = near.reshape(2, 2, TOK, HD)
    given = jnp.concatenate([quarter(1), near[1]]).reshape(4 * TOK, HD)
    came = swap(jnp.concatenate([packet.reshape(4 * (TOK + 16), HD), given]), "x", 1)
    far = came[4 * (TOK + 16) :].reshape(2, 2, TOK, HD)
    rows = jnp.concatenate([quarter(0), far[0], near[0], far[1]], axis=1)
    packet = jnp.stack([packet, came[: 4 * (TOK + 16)].reshape(4, TOK + 16, HD)])
    packet = jnp.concatenate([packet, swap(packet, "x", 3)])
    packet, weights = lax.optimization_barrier((packet, weights))
    packet = jnp.stack([packet, swap(packet, "core", 1)])

    kv = packet[:, :, :, :TOK].transpose(2, 0, 1, 3, 4).reshape(8, 4 * TOK, HD)
    total = jnp.sum(packet[:, :, :, TOK : TOK + 3].astype(jnp.float32), axis=(0, 2, 3))
    inv_all = lax.rsqrt(total / D + norm_eps)
    inv_scale = inv_all[0][:, None]
    gain_quarter = lax.dynamic_slice_in_dim(norm_gain, mine * QUARTER, QUARTER).reshape(2, 1, HD)
    normal = rows.astype(jnp.float32) * inv_all.reshape(1, 4 * TOK, 1)
    normed = (normal * gain_quarter).astype(jnp.bfloat16)

    products = jnp.einsum(
        "ktc,kbcf->kbtf",
        kv,
        weights,
        preferred_element_type=jnp.float32,
    ).astype(jnp.bfloat16)
    norm_grad = jnp.sum(products.astype(jnp.float32), axis=0)
    gain_part = terms_of(jnp.sum(norm_grad * normal, axis=1)).reshape(6, HD)

    pieces = jnp.einsum(
        "ktc,btf->kbcf", kv, normed, preferred_element_type=jnp.float32
    ).astype(jnp.bfloat16)
    gain_rows = jnp.broadcast_to(jnp.pad(gain_part, ((0, 10), (0, 0)))[None], (16, 16, HD))
    arrived = exchange(jnp.concatenate([pieces.reshape(16, HD, HD), gain_rows], axis=1), ROW)
    block = jnp.sum(arrived[:, :HD].astype(jnp.float32), axis=0)
    weight_grad = lax.ppermute(block, AXES, [(b, a) for a, b in moves])
    gains = jnp.sum(arrived[:, HD : HD + 6].astype(jnp.float32), axis=0)
    gains = jnp.sum(gains.reshape(3, 2, HD), axis=0)
    gains = exchange(jnp.broadcast_to(gains[None], (4, 2, HD)), "x")
    gain_grad = gains.reshape(4 * QUARTER)

    back = norm_grad.astype(jnp.bfloat16)
    near = swap(back[:, 2 * TOK :].reshape(4 * TOK, HD), "x", 3).reshape(2, 2 * TOK, HD)
    given = jnp.concatenate([back[:, TOK : 2 * TOK], near[:, TOK:]]).reshape(4 * TOK, HD)
    far = swap(given, "x", 1).reshape(2, 2, TOK, HD)

    full = jnp.zeros((8, TOK, HD), jnp.bfloat16)
    for part, r in ((back[:, :TOK], 0), (far[0], 1), (near[:, :TOK], 3), (far[1], 2)):
        full = lax.dynamic_update_slice_in_dim(full, part, (mine ^ r) * 2, axis=0)
    full = jnp.concatenate([full[i] for i in range(8)], axis=1)
    scaled = full.astype(jnp.float32) * norm_gain[None, :]
    normal = widened * inv_scale
    inner = jnp.sum(scaled * normal, axis=1)
    for axis, mask in (("core", 1), ("zl", 1), ("zl", 2)):
        inner = inner + swap(inner, axis, mask)
    inner = inner[:, None] / D
    input_grad = (
        residual_grad.astype(jnp.float32) + inv_scale * (scaled - normal * inner)
    ).astype(jnp.bfloat16)
    return (input_grad, weight_grad, gain_grad)


def solution(mesh):
    fine = Mesh(mesh.devices.reshape(SIZES), AXES)
    return jax.shard_map(
        shards,
        mesh=fine,
        in_specs=(
            P(DP, TENSOR),
            P(DP, TENSOR),
            P(DP, TENSOR),
            P(TENSOR, DP),
            P(TENSOR),
        ),
        out_specs=(P(DP, TENSOR), P(TENSOR, DP), P(TENSOR)),
        check_vma=False,
    )
```

```python
import jax
import jax.numpy as jnp
from jax import lax
from jax.sharding import Mesh
from jax.sharding import PartitionSpec as P

D = 8192
HD = 128
TOK = 128
QUARTER = 256

rope_theta = 500000.0
norm_eps = 1e-05

SIZES = (4, 8, 2, 4, 2)
AXES = ("x", "y", "zh", "zl", "core")
DP = ("x", "y", "zh")
TENSOR = ("zl", "core")
ROW = ("y", "zh")


def flat_index(x, y, zh, zl, core):
    return (((x * 8 + y) * 2 + zh) * 4 + zl) * 2 + core


def weight_moves():
    moves = []
    for x in range(4):
        for y in range(8):
            for zh in range(2):
                for zl in range(4):
                    for core in range(2):
                        far_zl, far_core = x, y // 4
                        place = (far_zl ^ zl) * 2 + (far_core ^ core)
                        there = flat_index(y % 4, place, zh, far_zl, far_core)
                        moves.append((flat_index(x, y, zh, zl, core), there))
    return moves


def exchange(value, axes):
    return lax.all_to_all(value, axes, split_axis=0, concat_axis=0, tiled=True)


def swap(value, axis, mask):
    count = lax.axis_size(axis)
    return lax.ppermute(value, axis, [(i, i ^ mask) for i in range(count)])


def terms_of(value):
    first = lax.reduce_precision(value, 8, 7)
    second = lax.reduce_precision(value - first, 8, 7)
    third = value - first - second
    return jnp.stack([first, second, third]).astype(jnp.bfloat16)


def rope_tables(positions_count, head_size):
    half_head = head_size // 2
    frequency = rope_theta ** (-(jnp.arange(half_head, dtype=jnp.float32) * 2.0 / head_size))
    angles = jnp.arange(positions_count, dtype=jnp.float32)[:, None] * frequency[None, :]
    return (jnp.cos(angles), jnp.sin(angles))


def shards(layer_input, residual_grad, key_value_grad, kv_weight, norm_gain):
    moves = weight_moves()
    mine = lax.axis_index("x")

    moved = lax.ppermute(kv_weight, AXES, moves)

    cosine, sine = rope_tables(TOK, HD)
    grads = key_value_grad.astype(jnp.float32)
    low, high = grads[:, : HD // 2], grads[:, HD // 2 :]
    turned = jnp.concatenate([low * cosine + high * sine, high * cosine - low * sine], axis=1)
    kv_pre = jnp.where(lax.axis_index("core") == 0, turned, grads).astype(jnp.bfloat16)
    widened = layer_input.astype(jnp.float32)
    squares = terms_of(jnp.sum(widened * widened, axis=1))
    packet = jnp.concatenate([kv_pre, jnp.pad(squares, ((0, 13), (0, 0)))], axis=0)[None]

    blocks = jnp.stack([layer_input[:, i * HD : (i + 1) * HD] for i in range(8)])

    def quarter(r):
        return lax.dynamic_slice_in_dim(blocks, (mine ^ r) * 2, 2, axis=0)

    packet, moved = lax.optimization_barrier((packet, moved))
    packet = jnp.concatenate([packet, swap(packet, "zl", 1)])
    weights = moved
    for axis, mask, place in (("zh", 1, 0), ("y", 4, 0), ("y", 2, 1), ("y", 1, 2)):
        other = swap(weights, axis, mask)
        first = (lax.axis_index(axis) & mask) == 0
        pair = [jnp.where(first, weights, other), jnp.where(first, other, weights)]
        weights = jnp.stack(pair, axis=place)
    weights = weights.reshape(8, 2, HD, HD)
    given = jnp.concatenate([quarter(3), quarter(2)]).reshape(4 * TOK, HD)
    near = swap(given, "x", 3)
    packet = jnp.concatenate([packet, swap(packet, "zl", 2)])
    packet, near = lax.optimization_barrier((packet, near))

    near = near.reshape(2, 2, TOK, HD)
    given = jnp.concatenate([quarter(1), near[1]]).reshape(4 * TOK, HD)
    came = swap(jnp.concatenate([packet.reshape(4 * (TOK + 16), HD), given]), "x", 1)
    far = came[4 * (TOK + 16) :].reshape(2, 2, TOK, HD)
    rows = jnp.concatenate([quarter(0), far[0], near[0], far[1]], axis=1)
    packet = jnp.stack([packet, came[: 4 * (TOK + 16)].reshape(4, TOK + 16, HD)])
    packet = jnp.concatenate([packet, swap(packet, "x", 3)])
    packet = jnp.stack([packet, swap(packet, "core", 1)])

    kv = packet[:, :, :, :TOK].transpose(2, 0, 1, 3, 4).reshape(8, 4 * TOK, HD)
    total = jnp.sum(packet[:, :, :, TOK : TOK + 3].astype(jnp.float32), axis=(0, 2, 3))
    inv_all = lax.rsqrt(total / D + norm_eps)
    inv_scale = inv_all[0][:, None]
    gain_quarter = lax.dynamic_slice_in_dim(norm_gain, mine * QUARTER, QUARTER).reshape(2, 1, HD)
    normal = rows.astype(jnp.float32) * inv_all.reshape(1, 4 * TOK, 1)
    normed = (normal * gain_quarter).astype(jnp.bfloat16)

    products = jnp.einsum(
        "ktc,kbcf->kbtf",
        kv,
        weights,
        preferred_element_type=jnp.float32,
    ).astype(jnp.bfloat16)
    norm_grad = jnp.sum(products.astype(jnp.float32), axis=0)
    gain_part = terms_of(jnp.sum(norm_grad * normal, axis=1)).reshape(6, HD)

    pieces = jnp.einsum(
        "ktc,btf->kbcf", kv, normed, preferred_element_type=jnp.float32
    ).astype(jnp.bfloat16)
    gain_rows = jnp.broadcast_to(jnp.pad(gain_part, ((0, 10), (0, 0)))[None], (16, 16, HD))
    arrived = exchange(jnp.concatenate([pieces.reshape(16, HD, HD), gain_rows], axis=1), ROW)
    block = jnp.sum(arrived[:, :HD].astype(jnp.float32), axis=0)
    weight_grad = lax.ppermute(block, AXES, [(b, a) for a, b in moves])
    gains = jnp.sum(arrived[:, HD : HD + 6].astype(jnp.float32), axis=0)
    gains = jnp.sum(gains.reshape(3, 2, HD), axis=0)
    gains = exchange(jnp.broadcast_to(gains[None], (4, 2, HD)), "x")
    gain_grad = gains.reshape(4 * QUARTER)

    back = norm_grad.astype(jnp.bfloat16)
    near = swap(back[:, 2 * TOK :].reshape(4 * TOK, HD), "x", 3).reshape(2, 2 * TOK, HD)
    given = jnp.concatenate([back[:, TOK : 2 * TOK], near[:, TOK:]]).reshape(4 * TOK, HD)
    far = swap(given, "x", 1).reshape(2, 2, TOK, HD)

    full = jnp.zeros((8, TOK, HD), jnp.bfloat16)
    for part, r in ((back[:, :TOK], 0), (far[0], 1), (near[:, :TOK], 3), (far[1], 2)):
        full = lax.dynamic_update_slice_in_dim(full, part, (mine ^ r) * 2, axis=0)
    full = jnp.concatenate([full[i] for i in range(8)], axis=1)
    scaled = full.astype(jnp.float32) * norm_gain[None, :]
    normal = widened * inv_scale
    inner = jnp.sum(scaled * normal, axis=1)
    for axis, mask in (("core", 1), ("zl", 1), ("zl", 2)):
        inner = inner + swap(inner, axis, mask)
    inner = inner[:, None] / D
    input_grad = (
        residual_grad.astype(jnp.float32) + inv_scale * (scaled - normal * inner)
    ).astype(jnp.bfloat16)
    return (input_grad, weight_grad, gain_grad)


def solution(mesh):
    fine = Mesh(mesh.devices.reshape(SIZES), AXES)
    return jax.shard_map(
        shards,
        mesh=fine,
        in_specs=(
            P(DP, TENSOR),
            P(DP, TENSOR),
            P(DP, TENSOR),
            P(TENSOR, DP),
            P(TENSOR),
        ),
        out_specs=(P(DP, TENSOR), P(TENSOR, DP), P(TENSOR)),
        check_vma=False,
    )
```

```python
import jax
import jax.numpy as jnp
from jax import lax
from jax.sharding import Mesh
from jax.sharding import PartitionSpec as P

D = 8192
HD = 128
TOK = 128
QUARTER = 256

rope_theta = 500000.0
norm_eps = 1e-05

SIZES = (4, 8, 2, 4, 2)
AXES = ("x", "y", "zh", "zl", "core")
DP = ("x", "y", "zh")
TENSOR = ("zl", "core")
ROW = ("y", "zh")


def flat_index(x, y, zh, zl, core):
    return (((x * 8 + y) * 2 + zh) * 4 + zl) * 2 + core


def weight_moves():
    moves = []
    for x in range(4):
        for y in range(8):
            for zh in range(2):
                for zl in range(4):
                    for core in range(2):
                        far_zl, far_core = x, y // 4
                        place = (far_zl ^ zl) * 2 + (far_core ^ core)
                        there = flat_index(y % 4, place, zh, far_zl, far_core)
                        moves.append((flat_index(x, y, zh, zl, core), there))
    return moves


def exchange(value, axes):
    return lax.all_to_all(value, axes, split_axis=0, concat_axis=0, tiled=True)


def swap(value, axis, mask):
    count = lax.axis_size(axis)
    return lax.ppermute(value, axis, [(i, i ^ mask) for i in range(count)])


def terms_of(value):
    first = lax.reduce_precision(value, 8, 7)
    second = lax.reduce_precision(value - first, 8, 7)
    third = value - first - second
    return jnp.stack([first, second, third]).astype(jnp.bfloat16)


def whole_of(terms):
    first, second, third = terms.astype(jnp.float32).reshape(3, 2, HD)
    return first + second + third


def rope_tables(positions_count, head_size):
    half_head = head_size // 2
    frequency = rope_theta ** (-(jnp.arange(half_head, dtype=jnp.float32) * 2.0 / head_size))
    angles = jnp.arange(positions_count, dtype=jnp.float32)[:, None] * frequency[None, :]
    return (jnp.cos(angles), jnp.sin(angles))


def shards(layer_input, residual_grad, key_value_grad, kv_weight, norm_gain):
    moves = weight_moves()
    mine = lax.axis_index("x")

    moved = lax.ppermute(kv_weight, AXES, moves)

    cosine, sine = rope_tables(TOK, HD)
    grads = key_value_grad.astype(jnp.float32)
    low, high = grads[:, : HD // 2], grads[:, HD // 2 :]
    turned = jnp.concatenate([low * cosine + high * sine, high * cosine - low * sine], axis=1)
    kv_pre = jnp.where(lax.axis_index("core") == 0, turned, grads).astype(jnp.bfloat16)
    widened = layer_input.astype(jnp.float32)
    squares = terms_of(jnp.sum(widened * widened, axis=1))
    packet = jnp.concatenate([kv_pre, jnp.pad(squares, ((0, 13), (0, 0)))], axis=0)[None]

    blocks = jnp.stack([layer_input[:, i * HD : (i + 1) * HD] for i in range(8)])

    def quarter(r):
        return lax.dynamic_slice_in_dim(blocks, (mine ^ r) * 2, 2, axis=0)

    packet, moved = lax.optimization_barrier((packet, moved))
    packet = jnp.concatenate([packet, swap(packet, "zl", 1)])
    weights = moved
    for axis, mask, place in (("zh", 1, 0), ("y", 4, 0), ("y", 2, 1), ("y", 1, 2)):
        other = swap(weights, axis, mask)
        first = (lax.axis_index(axis) & mask) == 0
        pair = [jnp.where(first, weights, other), jnp.where(first, other, weights)]
        weights = jnp.stack(pair, axis=place)
    weights = weights.reshape(8, 2, HD, HD)
    given = jnp.concatenate([quarter(3), quarter(2)]).reshape(4 * TOK, HD)
    near = swap(given, "x", 3)
    packet = jnp.concatenate([packet, swap(packet, "zl", 2)])
    packet, near = lax.optimization_barrier((packet, near))

    near = near.reshape(2, 2, TOK, HD)
    given = jnp.concatenate([quarter(1), near[1]]).reshape(4 * TOK, HD)
    came = swap(jnp.concatenate([packet.reshape(4 * (TOK + 16), HD), given]), "x", 1)
    far = came[4 * (TOK + 16) :].reshape(2, 2, TOK, HD)
    rows = jnp.concatenate([quarter(0), far[0], near[0], far[1]], axis=1)
    packet = jnp.stack([packet, came[: 4 * (TOK + 16)].reshape(4, TOK + 16, HD)])
    packet = jnp.concatenate([packet, swap(packet, "x", 3)])
    packet = jnp.stack([packet, swap(packet, "core", 1)])

    kv = packet[:, :, :, :TOK].transpose(2, 0, 1, 3, 4).reshape(8, 4 * TOK, HD)
    total = jnp.sum(packet[:, :, :, TOK : TOK + 3].astype(jnp.float32), axis=(0, 2, 3))
    inv_all = lax.rsqrt(total / D + norm_eps)
    inv_scale = inv_all[0][:, None]
    gain_quarter = lax.dynamic_slice_in_dim(norm_gain, mine * QUARTER, QUARTER).reshape(2, 1, HD)
    normal = rows.astype(jnp.float32) * inv_all.reshape(1, 4 * TOK, 1)
    normed = (normal * gain_quarter).astype(jnp.bfloat16)

    products = jnp.einsum(
        "ktc,kbcf->kbtf",
        kv,
        weights,
        preferred_element_type=jnp.float32,
    ).astype(jnp.bfloat16)
    norm_grad = jnp.sum(products.astype(jnp.float32), axis=0)
    gain_sum = jnp.sum(norm_grad * normal, axis=1)

    back = norm_grad.astype(jnp.bfloat16)
    near = swap(back[:, 2 * TOK :].reshape(4 * TOK, HD), "x", 3)

    sums = jnp.einsum("ktc,btf->kbcf", kv, normed, preferred_element_type=jnp.float32)
    sums = sums.reshape(2, 2, 2, 2, HD, HD)
    for mask, place in ((1, 2), (2, 1), (4, 0)):
        first = (lax.axis_index("y") & mask) == 0
        low, high = (lax.index_in_dim(sums, i, place, keepdims=False) for i in range(2))
        given = jnp.where(first, high, low).astype(jnp.bfloat16).reshape(-1, HD)
        terms = terms_of(gain_sum).reshape(6, HD)
        came = swap(jnp.concatenate([given, jnp.pad(terms, ((0, 10), (0, 0)))]), "y", mask)
        if mask == 1:
            near, came = lax.optimization_barrier((near, came))
        kept = jnp.where(first, low, high)
        sums = kept + came[:-16].astype(jnp.float32).reshape(kept.shape)
        gain_sum = whole_of(terms) + whole_of(came[-16:-10])
    first = lax.axis_index("zh") == 0
    given = jnp.where(first, sums[1], sums[0])
    came = swap(jnp.concatenate([given, jnp.pad(gain_sum, ((0, 6), (0, 0)))]), "zh", 1)
    block = jnp.where(first, sums[0], sums[1]) + came[:HD]
    gain_sum = gain_sum + came[HD : HD + 2]
    weight_grad = lax.ppermute(block, AXES, [(b, a) for a, b in moves])
    gain_sum, block = lax.optimization_barrier((gain_sum, block))
    gains = exchange(jnp.broadcast_to(gain_sum[None], (4, 2, HD)), "x")
    gain_grad = gains.reshape(4 * QUARTER)

    near = near.reshape(2, 2 * TOK, HD)
    given = jnp.concatenate([back[:, TOK : 2 * TOK], near[:, TOK:]]).reshape(4 * TOK, HD)
    far = swap(given, "x", 1).reshape(2, 2, TOK, HD)

    full = jnp.zeros((8, TOK, HD), jnp.bfloat16)
    for part, r in ((back[:, :TOK], 0), (far[0], 1), (near[:, :TOK], 3), (far[1], 2)):
        full = lax.dynamic_update_slice_in_dim(full, part, (mine ^ r) * 2, axis=0)
    full = jnp.concatenate([full[i] for i in range(8)], axis=1)
    scaled = full.astype(jnp.float32) * norm_gain[None, :]
    normal = widened * inv_scale
    inner = jnp.sum(scaled * normal, axis=1)
    for axis, mask in (("core", 1), ("zl", 1), ("zl", 2)):
        inner = inner + swap(inner, axis, mask)
    inner = inner[:, None] / D
    input_grad = (
        residual_grad.astype(jnp.float32) + inv_scale * (scaled - normal * inner)
    ).astype(jnp.bfloat16)
    return (input_grad, weight_grad, gain_grad)


def solution(mesh):
    fine = Mesh(mesh.devices.reshape(SIZES), AXES)
    return jax.shard_map(
        shards,
        mesh=fine,
        in_specs=(
            P(DP, TENSOR),
            P(DP, TENSOR),
            P(DP, TENSOR),
            P(TENSOR, DP),
            P(TENSOR),
        ),
        out_specs=(P(DP, TENSOR), P(TENSOR, DP), P(TENSOR)),
        check_vma=False,
    )
```

```python
import jax
import jax.numpy as jnp
from jax import lax
from jax.sharding import Mesh
from jax.sharding import PartitionSpec as P

D = 8192
HD = 128
TOK = 128
QUARTER = 256

rope_theta = 500000.0
norm_eps = 1e-05

SIZES = (4, 8, 2, 4, 2)
AXES = ("x", "y", "zh", "zl", "core")
DP = ("x", "y", "zh")
TENSOR = ("zl", "core")
ROW = ("y", "zh")


def flat_index(x, y, zh, zl, core):
    return (((x * 8 + y) * 2 + zh) * 4 + zl) * 2 + core


def weight_moves():
    moves = []
    for x in range(4):
        for y in range(8):
            for zh in range(2):
                for zl in range(4):
                    for core in range(2):
                        far_zl, far_core = x, y // 4
                        place = (far_zl ^ zl) * 2 + (far_core ^ core)
                        there = flat_index(y % 4, place, zh, far_zl, far_core)
                        moves.append((flat_index(x, y, zh, zl, core), there))
    return moves


def exchange(value, axes):
    return lax.all_to_all(value, axes, split_axis=0, concat_axis=0, tiled=True)


def swap(value, axis, mask):
    count = lax.axis_size(axis)
    return lax.ppermute(value, axis, [(i, i ^ mask) for i in range(count)])


def terms_of(value):
    first = lax.reduce_precision(value, 8, 7)
    second = lax.reduce_precision(value - first, 8, 7)
    third = value - first - second
    return jnp.stack([first, second, third]).astype(jnp.bfloat16)


def rope_tables(positions_count, head_size):
    half_head = head_size // 2
    frequency = rope_theta ** (-(jnp.arange(half_head, dtype=jnp.float32) * 2.0 / head_size))
    angles = jnp.arange(positions_count, dtype=jnp.float32)[:, None] * frequency[None, :]
    return (jnp.cos(angles), jnp.sin(angles))


def shards(layer_input, residual_grad, key_value_grad, kv_weight, norm_gain):
    moves = weight_moves()
    mine = lax.axis_index("x")

    moved = lax.ppermute(kv_weight, AXES, moves)

    cosine, sine = rope_tables(TOK, HD)
    grads = key_value_grad.astype(jnp.float32)
    low, high = grads[:, : HD // 2], grads[:, HD // 2 :]
    turned = jnp.concatenate([low * cosine + high * sine, high * cosine - low * sine], axis=1)
    kv_pre = jnp.where(lax.axis_index("core") == 0, turned, grads).astype(jnp.bfloat16)
    widened = layer_input.astype(jnp.float32)
    squares = terms_of(jnp.sum(widened * widened, axis=1))
    packet = jnp.concatenate([kv_pre, jnp.pad(squares, ((0, 13), (0, 0)))], axis=0)[None]

    blocks = jnp.stack([layer_input[:, i * HD : (i + 1) * HD] for i in range(8)])

    def quarter(r):
        return lax.dynamic_slice_in_dim(blocks, (mine ^ r) * 2, 2, axis=0)

    given = jnp.concatenate([quarter(3), quarter(2)]).reshape(4 * TOK, HD)
    near = swap(given, "x", 3)
    packet, moved, near = lax.optimization_barrier((packet, moved, near))
    packet = jnp.concatenate([packet, swap(packet, "zl", 1)])
    weights = moved
    for axis, mask, place in (("zh", 1, 0), ("y", 4, 0), ("y", 2, 1), ("y", 1, 2)):
        other = swap(weights, axis, mask)
        first = (lax.axis_index(axis) & mask) == 0
        pair = [jnp.where(first, weights, other), jnp.where(first, other, weights)]
        weights = jnp.stack(pair, axis=place)
    weights = weights.reshape(8, 2, HD, HD)
    packet = jnp.concatenate([packet, swap(packet, "zl", 2)])

    near = near.reshape(2, 2, TOK, HD)
    given = jnp.concatenate([quarter(1), near[1]]).reshape(4 * TOK, HD)
    came = swap(jnp.concatenate([packet.reshape(4 * (TOK + 16), HD), given]), "x", 1)
    far = came[4 * (TOK + 16) :].reshape(2, 2, TOK, HD)
    rows = jnp.concatenate([quarter(0), far[0], near[0], far[1]], axis=1)
    packet = jnp.stack([packet, came[: 4 * (TOK + 16)].reshape(4, TOK + 16, HD)])
    packet = jnp.concatenate([packet, swap(packet, "x", 3)])
    packet = jnp.stack([packet, swap(packet, "core", 1)])

    kv = packet[:, :, :, :TOK].transpose(2, 0, 1, 3, 4).reshape(8, 4 * TOK, HD)
    total = jnp.sum(packet[:, :, :, TOK : TOK + 3].astype(jnp.float32), axis=(0, 2, 3))
    inv_all = lax.rsqrt(total / D + norm_eps)
    inv_scale = inv_all[0][:, None]
    gain_quarter = lax.dynamic_slice_in_dim(norm_gain, mine * QUARTER, QUARTER).reshape(2, 1, HD)
    normal = rows.astype(jnp.float32) * inv_all.reshape(1, 4 * TOK, 1)
    normed = (normal * gain_quarter).astype(jnp.bfloat16)

    products = jnp.einsum(
        "ktc,kbcf->kbtf",
        kv,
        weights,
        preferred_element_type=jnp.float32,
    ).astype(jnp.bfloat16)
    norm_grad = jnp.sum(products.astype(jnp.float32), axis=0)
    gain_part = terms_of(jnp.sum(norm_grad * normal, axis=1)).reshape(6, HD)

    pieces = jnp.einsum(
        "ktc,btf->kbcf", kv, normed, preferred_element_type=jnp.float32
    ).astype(jnp.bfloat16)
    gain_rows = jnp.broadcast_to(jnp.pad(gain_part, ((0, 10), (0, 0)))[None], (16, 16, HD))
    arrived = exchange(jnp.concatenate([pieces.reshape(16, HD, HD), gain_rows], axis=1), ROW)
    back = norm_grad.astype(jnp.bfloat16)
    near = swap(back[:, 2 * TOK :].reshape(4 * TOK, HD), "x", 3).reshape(2, 2 * TOK, HD)
    given = jnp.concatenate([back[:, TOK : 2 * TOK], near[:, TOK:]]).reshape(4 * TOK, HD)
    far = swap(given, "x", 1).reshape(2, 2, TOK, HD)

    full = jnp.zeros((8, TOK, HD), jnp.bfloat16)
    for part, r in ((back[:, :TOK], 0), (far[0], 1), (near[:, :TOK], 3), (far[1], 2)):
        full = lax.dynamic_update_slice_in_dim(full, part, (mine ^ r) * 2, axis=0)
    full = jnp.concatenate([full[i] for i in range(8)], axis=1)
    scaled = full.astype(jnp.float32) * norm_gain[None, :]
    normal = widened * inv_scale
    inner = jnp.sum(scaled * normal, axis=1)
    block = jnp.sum(arrived[:, :HD].astype(jnp.float32), axis=0)
    gains = jnp.sum(arrived[:, HD : HD + 6].astype(jnp.float32), axis=0)
    gains = jnp.sum(gains.reshape(3, 2, HD), axis=0)
    inner, gains, block = lax.optimization_barrier((inner, gains, block))
    weight_grad = lax.ppermute(block, AXES, [(b, a) for a, b in moves])
    inner = inner + swap(inner, "core", 1)
    both = jnp.concatenate([inner[None], gains])
    both = exchange(jnp.broadcast_to(both[None], (16, 3, HD)), ("x", "zl")).reshape(4, 4, 3, HD)
    both, weight_grad = lax.optimization_barrier((both, weight_grad))
    inner = lax.dynamic_index_in_dim(both[:, :, 0], mine, 0, keepdims=False)
    inner = jnp.sum(inner, axis=0)[:, None] / D
    gains = lax.dynamic_index_in_dim(both[:, :, 1:], lax.axis_index("zl"), 1, keepdims=False)
    gain_grad = gains.reshape(4 * QUARTER)
    input_grad = (
        residual_grad.astype(jnp.float32) + inv_scale * (scaled - normal * inner)
    ).astype(jnp.bfloat16)
    return (input_grad, weight_grad, gain_grad)


def solution(mesh):
    fine = Mesh(mesh.devices.reshape(SIZES), AXES)
    return jax.shard_map(
        shards,
        mesh=fine,
        in_specs=(
            P(DP, TENSOR),
            P(DP, TENSOR),
            P(DP, TENSOR),
            P(TENSOR, DP),
            P(TENSOR),
        ),
        out_specs=(P(DP, TENSOR), P(TENSOR, DP), P(TENSOR)),
        check_vma=False,
    )
```

```python
import jax
import jax.numpy as jnp
from jax import lax
from jax.sharding import Mesh
from jax.sharding import PartitionSpec as P

D = 8192
HD = 128
TOK = 128
QUARTER = 256

rope_theta = 500000.0
norm_eps = 1e-05

SIZES = (4, 8, 2, 4, 2)
AXES = ("x", "y", "zh", "zl", "core")
DP = ("x", "y", "zh")
TENSOR = ("zl", "core")
ROW = ("y", "zh")


def flat_index(x, y, zh, zl, core):
    return (((x * 8 + y) * 2 + zh) * 4 + zl) * 2 + core


def weight_moves():
    moves = []
    for x in range(4):
        for y in range(8):
            for zh in range(2):
                for zl in range(4):
                    for core in range(2):
                        far_zl, far_core = x, y // 4
                        place = (far_zl ^ zl) * 2 + (far_core ^ core)
                        there = flat_index(y % 4, place, zh, far_zl, far_core)
                        moves.append((flat_index(x, y, zh, zl, core), there))
    return moves


def exchange(value, axes):
    return lax.all_to_all(value, axes, split_axis=0, concat_axis=0, tiled=True)


def swap(value, axis, mask):
    count = lax.axis_size(axis)
    return lax.ppermute(value, axis, [(i, i ^ mask) for i in range(count)])


def terms_of(value):
    first = lax.reduce_precision(value, 8, 7)
    second = lax.reduce_precision(value - first, 8, 7)
    third = value - first - second
    return jnp.stack([first, second, third]).astype(jnp.bfloat16)


def rope_tables(positions_count, head_size):
    half_head = head_size // 2
    frequency = rope_theta ** (-(jnp.arange(half_head, dtype=jnp.float32) * 2.0 / head_size))
    angles = jnp.arange(positions_count, dtype=jnp.float32)[:, None] * frequency[None, :]
    return (jnp.cos(angles), jnp.sin(angles))


def shards(layer_input, residual_grad, key_value_grad, kv_weight, norm_gain):
    moves = weight_moves()
    mine = lax.axis_index("x")

    moved = lax.ppermute(kv_weight, AXES, moves)
    other = lax.ppermute(kv_weight, AXES, [(a, b ^ 8) for a, b in moves])

    cosine, sine = rope_tables(TOK, HD)
    grads = key_value_grad.astype(jnp.float32)
    low, high = grads[:, : HD // 2], grads[:, HD // 2 :]
    turned = jnp.concatenate([low * cosine + high * sine, high * cosine - low * sine], axis=1)
    kv_pre = jnp.where(lax.axis_index("core") == 0, turned, grads).astype(jnp.bfloat16)
    widened = layer_input.astype(jnp.float32)
    squares = terms_of(jnp.sum(widened * widened, axis=1))
    packet = jnp.concatenate([kv_pre, jnp.pad(squares, ((0, 13), (0, 0)))], axis=0)[None]

    blocks = jnp.stack([layer_input[:, i * HD : (i + 1) * HD] for i in range(8)])

    def quarter(r):
        return lax.dynamic_slice_in_dim(blocks, (mine ^ r) * 2, 2, axis=0)

    packet, moved, other = lax.optimization_barrier((packet, moved, other))
    packet = jnp.concatenate([packet, swap(packet, "zl", 1)])
    first = lax.axis_index("zh") == 0
    weights = jnp.stack([jnp.where(first, moved, other), jnp.where(first, other, moved)])
    for mask, place in ((4, 0), (2, 1), (1, 2)):
        other = swap(weights, "y", mask)
        first = (lax.axis_index("y") & mask) == 0
        pair = [jnp.where(first, weights, other), jnp.where(first, other, weights)]
        weights = jnp.stack(pair, axis=place)
    weights = weights.reshape(8, 2, HD, HD)
    given = jnp.concatenate([quarter(3), quarter(2)]).reshape(4 * TOK, HD)
    near = swap(given, "x", 3)
    packet = jnp.concatenate([packet, swap(packet, "zl", 2)])
    packet, near = lax.optimization_barrier((packet, near))

    near = near.reshape(2, 2, TOK, HD)
    given = jnp.concatenate([quarter(1), near[1]]).reshape(4 * TOK, HD)
    came = swap(jnp.concatenate([packet.reshape(4 * (TOK + 16), HD), given]), "x", 1)
    far = came[4 * (TOK + 16) :].reshape(2, 2, TOK, HD)
    rows = jnp.concatenate([quarter(0), far[0], near[0], far[1]], axis=1)
    packet = jnp.stack([packet, came[: 4 * (TOK + 16)].reshape(4, TOK + 16, HD)])
    packet = jnp.concatenate([packet, swap(packet, "x", 3)])
    packet = jnp.stack([packet, swap(packet, "core", 1)])

    kv = packet[:, :, :, :TOK].transpose(2, 0, 1, 3, 4).reshape(8, 4 * TOK, HD)
    total = jnp.sum(packet[:, :, :, TOK : TOK + 3].astype(jnp.float32), axis=(0, 2, 3))
    inv_all = lax.rsqrt(total / D + norm_eps)
    inv_scale = inv_all[0][:, None]
    gain_quarter = lax.dynamic_slice_in_dim(norm_gain, mine * QUARTER, QUARTER).reshape(2, 1, HD)
    normal = rows.astype(jnp.float32) * inv_all.reshape(1, 4 * TOK, 1)
    normed = (normal * gain_quarter).astype(jnp.bfloat16)

    products = jnp.einsum(
        "ktc,kbcf->kbtf",
        kv,
        weights,
        preferred_element_type=jnp.float32,
    ).astype(jnp.bfloat16)
    norm_grad = jnp.sum(products.astype(jnp.float32), axis=0)
    gain_part = terms_of(jnp.sum(norm_grad * normal, axis=1)).reshape(6, HD)

    pieces = jnp.einsum(
        "ktc,btf->kbcf", kv, normed, preferred_element_type=jnp.float32
    ).astype(jnp.bfloat16)
    gain_rows = jnp.broadcast_to(jnp.pad(gain_part, ((0, 2), (0, 0)))[None], (16, 8, HD))
    arrived = exchange(jnp.concatenate([pieces.reshape(16, HD, HD), gain_rows], axis=1), ROW)
    back = norm_grad.astype(jnp.bfloat16)
    near = swap(back[:, 2 * TOK :].reshape(4 * TOK, HD), "x", 3).reshape(2, 2 * TOK, HD)
    given = jnp.concatenate([back[:, TOK : 2 * TOK], near[:, TOK:]]).reshape(4 * TOK, HD)
    far = swap(given, "x", 1).reshape(2, 2, TOK, HD)

    full = jnp.zeros((8, TOK, HD), jnp.bfloat16)
    for part, r in ((back[:, :TOK], 0), (far[0], 1), (near[:, :TOK], 3), (far[1], 2)):
        full = lax.dynamic_update_slice_in_dim(full, part, (mine ^ r) * 2, axis=0)
    full = jnp.concatenate([full[i] for i in range(8)], axis=1)
    scaled = full.astype(jnp.float32) * norm_gain[None, :]
    normal = widened * inv_scale
    inner = jnp.sum(scaled * normal, axis=1)
    block = jnp.sum(arrived[:, :HD].astype(jnp.float32), axis=0)
    gains = jnp.sum(arrived[:, HD : HD + 6].astype(jnp.float32), axis=0)
    gains = jnp.sum(gains.reshape(3, 2, HD), axis=0)
    inner, gains, block = lax.optimization_barrier((inner, gains, block))
    weight_grad = lax.ppermute(block, AXES, [(b, a) for a, b in moves])
    inner = inner + swap(inner, "core", 1)
    both = jnp.concatenate([inner[None], gains])
    both = exchange(jnp.broadcast_to(both[None], (16, 3, HD)), ("x", "zl")).reshape(4, 4, 3, HD)
    both, weight_grad = lax.optimization_barrier((both, weight_grad))
    inner = lax.dynamic_index_in_dim(both[:, :, 0], mine, 0, keepdims=False)
    inner = jnp.sum(inner, axis=0)[:, None] / D
    gains = lax.dynamic_index_in_dim(both[:, :, 1:], lax.axis_index("zl"), 1, keepdims=False)
    gain_grad = gains.reshape(4 * QUARTER)
    input_grad = (
        residual_grad.astype(jnp.float32) + inv_scale * (scaled - normal * inner)
    ).astype(jnp.bfloat16)
    return (input_grad, weight_grad, gain_grad)


def solution(mesh):
    fine = Mesh(mesh.devices.reshape(SIZES), AXES)
    return jax.shard_map(
        shards,
        mesh=fine,
        in_specs=(
            P(DP, TENSOR),
            P(DP, TENSOR),
            P(DP, TENSOR),
            P(TENSOR, DP),
            P(TENSOR),
        ),
        out_specs=(P(DP, TENSOR), P(TENSOR, DP), P(TENSOR)),
        check_vma=False,
    )
```

```python
import jax
import jax.numpy as jnp
from jax import lax
from jax.sharding import Mesh
from jax.sharding import PartitionSpec as P

D = 8192
HD = 128
TOK = 128
QUARTER = 256

rope_theta = 500000.0
norm_eps = 1e-05

SIZES = (4, 8, 2, 4, 2)
AXES = ("x", "y", "zh", "zl", "core")
DP = ("x", "y", "zh")
TENSOR = ("zl", "core")
ROW = ("y", "zh")


def flat_index(x, y, zh, zl, core):
    return (((x * 8 + y) * 2 + zh) * 4 + zl) * 2 + core


def weight_moves():
    moves = []
    for x in range(4):
        for y in range(8):
            for zh in range(2):
                for zl in range(4):
                    for core in range(2):
                        far_zl, far_core = x, y // 4
                        place = (far_zl ^ zl) * 2 + (far_core ^ core)
                        there = flat_index(y % 4, place, zh, far_zl, far_core)
                        moves.append((flat_index(x, y, zh, zl, core), there))
    return moves


def exchange(value, axes):
    return lax.all_to_all(value, axes, split_axis=0, concat_axis=0, tiled=True)


def swap(value, axis, mask):
    count = lax.axis_size(axis)
    return lax.ppermute(value, axis, [(i, i ^ mask) for i in range(count)])


def terms_of(value):
    first = lax.reduce_precision(value, 8, 7)
    second = lax.reduce_precision(value - first, 8, 7)
    third = value - first - second
    return jnp.stack([first, second, third]).astype(jnp.bfloat16)


def rope_tables(positions_count, head_size):
    half_head = head_size // 2
    frequency = rope_theta ** (-(jnp.arange(half_head, dtype=jnp.float32) * 2.0 / head_size))
    angles = jnp.arange(positions_count, dtype=jnp.float32)[:, None] * frequency[None, :]
    return (jnp.cos(angles), jnp.sin(angles))


def shards(layer_input, residual_grad, key_value_grad, kv_weight, norm_gain):
    moves = weight_moves()
    mine = lax.axis_index("x")

    moved = lax.ppermute(kv_weight, AXES, moves)
    other = lax.ppermute(kv_weight, AXES, [(a, b ^ 8) for a, b in moves])

    cosine, sine = rope_tables(TOK, HD)
    grads = key_value_grad.astype(jnp.float32)
    low, high = grads[:, : HD // 2], grads[:, HD // 2 :]
    turned = jnp.concatenate([low * cosine + high * sine, high * cosine - low * sine], axis=1)
    kv_pre = jnp.where(lax.axis_index("core") == 0, turned, grads).astype(jnp.bfloat16)
    widened = layer_input.astype(jnp.float32)
    squares = terms_of(jnp.sum(widened * widened, axis=1))
    packet = jnp.concatenate([kv_pre, jnp.pad(squares, ((0, 13), (0, 0)))], axis=0)[None]

    blocks = jnp.stack([layer_input[:, i * HD : (i + 1) * HD] for i in range(8)])

    def quarter(r):
        return lax.dynamic_slice_in_dim(blocks, (mine ^ r) * 2, 2, axis=0)

    packet = jnp.concatenate([packet, swap(packet, "zl", 1)])
    packet, moved, other = lax.optimization_barrier((packet, moved, other))
    first = lax.axis_index("zh") == 0
    weights = jnp.stack([jnp.where(first, moved, other), jnp.where(first, other, moved)])
    for mask, place in ((4, 0), (2, 1), (1, 2)):
        other = swap(weights, "y", mask)
        first = (lax.axis_index("y") & mask) == 0
        pair = [jnp.where(first, weights, other), jnp.where(first, other, weights)]
        weights = jnp.stack(pair, axis=place)
    weights = weights.reshape(8, 2, HD, HD)
    given = jnp.concatenate([quarter(3), quarter(2)]).reshape(4 * TOK, HD)
    near = swap(given, "x", 3)
    packet = jnp.concatenate([packet, swap(packet, "zl", 2)])
    packet, near = lax.optimization_barrier((packet, near))

    near = near.reshape(2, 2, TOK, HD)
    given = jnp.concatenate([quarter(1), near[1]]).reshape(4 * TOK, HD)
    came = swap(jnp.concatenate([packet.reshape(4 * (TOK + 16), HD), given]), "x", 1)
    far = came[4 * (TOK + 16) :].reshape(2, 2, TOK, HD)
    rows = jnp.concatenate([quarter(0), far[0], near[0], far[1]], axis=1)
    packet = jnp.stack([packet, came[: 4 * (TOK + 16)].reshape(4, TOK + 16, HD)])
    packet = jnp.concatenate([packet, swap(packet, "x", 3)])
    packet = jnp.stack([packet, swap(packet, "core", 1)])

    kv = packet[:, :, :, :TOK].transpose(2, 0, 1, 3, 4).reshape(8, 4 * TOK, HD)
    total = jnp.sum(packet[:, :, :, TOK : TOK + 3].astype(jnp.float32), axis=(0, 2, 3))
    inv_all = lax.rsqrt(total / D + norm_eps)
    inv_scale = inv_all[0][:, None]
    gain_quarter = lax.dynamic_slice_in_dim(norm_gain, mine * QUARTER, QUARTER).reshape(2, 1, HD)
    normal = rows.astype(jnp.float32) * inv_all.reshape(1, 4 * TOK, 1)
    normed = (normal * gain_quarter).astype(jnp.bfloat16)

    products = jnp.einsum(
        "ktc,kbcf->kbtf",
        kv,
        weights,
        preferred_element_type=jnp.float32,
    ).astype(jnp.bfloat16)
    norm_grad = jnp.sum(products.astype(jnp.float32), axis=0)
    gain_part = terms_of(jnp.sum(norm_grad * normal, axis=1)).reshape(6, HD)

    pieces = jnp.einsum(
        "ktc,btf->kbcf", kv, normed, preferred_element_type=jnp.float32
    ).astype(jnp.bfloat16)
    gain_rows = jnp.broadcast_to(jnp.pad(gain_part, ((0, 2), (0, 0)))[None], (16, 8, HD))
    arrived = exchange(jnp.concatenate([pieces.reshape(16, HD, HD), gain_rows], axis=1), ROW)
    block = jnp.sum(arrived[:, :HD].astype(jnp.float32), axis=0)
    weight_grad = lax.ppermute(block, AXES, [(b, a) for a, b in moves])
    gains = jnp.sum(arrived[:, HD : HD + 6].astype(jnp.float32), axis=0)
    gains = jnp.sum(gains.reshape(3, 2, HD), axis=0)
    gains = exchange(jnp.broadcast_to(gains[None], (4, 2, HD)), "x")
    gain_grad = gains.reshape(4 * QUARTER)

    back = norm_grad.astype(jnp.bfloat16)
    near = swap(back[:, 2 * TOK :].reshape(4 * TOK, HD), "x", 3).reshape(2, 2 * TOK, HD)
    given = jnp.concatenate([back[:, TOK : 2 * TOK], near[:, TOK:]]).reshape(4 * TOK, HD)
    far = swap(given, "x", 1).reshape(2, 2, TOK, HD)

    full = jnp.zeros((8, TOK, HD), jnp.bfloat16)
    for part, r in ((back[:, :TOK], 0), (far[0], 1), (near[:, :TOK], 3), (far[1], 2)):
        full = lax.dynamic_update_slice_in_dim(full, part, (mine ^ r) * 2, axis=0)
    full = jnp.concatenate([full[i] for i in range(8)], axis=1)
    scaled = full.astype(jnp.float32) * norm_gain[None, :]
    normal = widened * inv_scale
    inner = jnp.sum(scaled * normal, axis=1)
    for axis, mask in (("core", 1), ("zl", 1), ("zl", 2)):
        inner = inner + swap(inner, axis, mask)
    inner = inner[:, None] / D
    input_grad = (
        residual_grad.astype(jnp.float32) + inv_scale * (scaled - normal * inner)
    ).astype(jnp.bfloat16)
    return (input_grad, weight_grad, gain_grad)


def solution(mesh):
    fine = Mesh(mesh.devices.reshape(SIZES), AXES)
    return jax.shard_map(
        shards,
        mesh=fine,
        in_specs=(
            P(DP, TENSOR),
            P(DP, TENSOR),
            P(DP, TENSOR),
            P(TENSOR, DP),
            P(TENSOR),
        ),
        out_specs=(P(DP, TENSOR), P(TENSOR, DP), P(TENSOR)),
        check_vma=False,
    )
```

```python
import jax
import jax.numpy as jnp
from jax import lax
from jax.sharding import Mesh
from jax.sharding import PartitionSpec as P

D = 8192
HD = 128
TOK = 128
QUARTER = 256

rope_theta = 500000.0
norm_eps = 1e-05

SIZES = (4, 8, 2, 4, 2)
AXES = ("x", "y", "zh", "zl", "core")
DP = ("x", "y", "zh")
TENSOR = ("zl", "core")


def flat_index(x, y, zh, zl, core):
    return (((x * 8 + y) * 2 + zh) * 4 + zl) * 2 + core


def weight_moves():
    moves = []
    for x in range(4):
        for y in range(8):
            for zh in range(2):
                for zl in range(4):
                    for core in range(2):
                        far_zl, far_core = x, y // 4
                        place = (far_zl ^ zl) * 2 + (far_core ^ core)
                        there = flat_index(y % 4, place, zh, far_zl, far_core)
                        moves.append((flat_index(x, y, zh, zl, core), there))
    return moves


def exchange(value, axes):
    return lax.all_to_all(value, axes, split_axis=0, concat_axis=0, tiled=True)


def swap(value, axis, mask):
    count = lax.axis_size(axis)
    return lax.ppermute(value, axis, [(i, i ^ mask) for i in range(count)])


def terms_of(value):
    first = lax.reduce_precision(value, 8, 7)
    second = lax.reduce_precision(value - first, 8, 7)
    third = value - first - second
    return jnp.stack([first, second, third]).astype(jnp.bfloat16)


def whole_of(terms):
    first, second, third = terms.astype(jnp.float32).reshape(3, 2, HD)
    return first + second + third


def rope_tables(positions_count, head_size):
    half_head = head_size // 2
    frequency = rope_theta ** (-(jnp.arange(half_head, dtype=jnp.float32) * 2.0 / head_size))
    angles = jnp.arange(positions_count, dtype=jnp.float32)[:, None] * frequency[None, :]
    return (jnp.cos(angles), jnp.sin(angles))


def shards(layer_input, residual_grad, key_value_grad, kv_weight, norm_gain):
    moves = weight_moves()
    mine = lax.axis_index("x")

    moved = lax.ppermute(kv_weight, AXES, moves)
    other = lax.ppermute(kv_weight, AXES, [(a, b ^ 8) for a, b in moves])

    cosine, sine = rope_tables(TOK, HD)
    grads = key_value_grad.astype(jnp.float32)
    low, high = grads[:, : HD // 2], grads[:, HD // 2 :]
    turned = jnp.concatenate([low * cosine + high * sine, high * cosine - low * sine], axis=1)
    kv_pre = jnp.where(lax.axis_index("core") == 0, turned, grads).astype(jnp.bfloat16)
    widened = layer_input.astype(jnp.float32)
    squares = terms_of(jnp.sum(widened * widened, axis=1))
    packet = jnp.concatenate([kv_pre, jnp.pad(squares, ((0, 13), (0, 0)))], axis=0)[None]

    blocks = jnp.stack([layer_input[:, i * HD : (i + 1) * HD] for i in range(8)])

    def quarter(r):
        return lax.dynamic_slice_in_dim(blocks, (mine ^ r) * 2, 2, axis=0)

    packet = jnp.concatenate([packet, swap(packet, "zl", 1)])
    packet, moved, other = lax.optimization_barrier((packet, moved, other))
    first = lax.axis_index("zh") == 0
    weights = jnp.stack([jnp.where(first, moved, other), jnp.where(first, other, moved)])
    for mask, place in ((4, 0), (2, 1), (1, 2)):
        other = swap(weights, "y", mask)
        first = (lax.axis_index("y") & mask) == 0
        pair = [jnp.where(first, weights, other), jnp.where(first, other, weights)]
        weights = jnp.stack(pair, axis=place)
    weights = weights.reshape(8, 2, HD, HD)
    given = jnp.concatenate([quarter(3), quarter(2)]).reshape(4 * TOK, HD)
    near = swap(given, "x", 3)
    packet = jnp.concatenate([packet, swap(packet, "zl", 2)])
    packet, near = lax.optimization_barrier((packet, near))

    near = near.reshape(2, 2, TOK, HD)
    given = jnp.concatenate([quarter(1), near[1]]).reshape(4 * TOK, HD)
    came = swap(jnp.concatenate([packet.reshape(4 * (TOK + 16), HD), given]), "x", 1)
    far = came[4 * (TOK + 16) :].reshape(2, 2, TOK, HD)
    rows = jnp.concatenate([quarter(0), far[0], near[0], far[1]], axis=1)
    packet = jnp.stack([packet, came[: 4 * (TOK + 16)].reshape(4, TOK + 16, HD)])
    packet = jnp.concatenate([packet, swap(packet, "x", 3)])
    packet = jnp.stack([packet, swap(packet, "core", 1)])

    kv = packet[:, :, :, :TOK].transpose(2, 0, 1, 3, 4).reshape(8, 4 * TOK, HD)
    total = jnp.sum(packet[:, :, :, TOK : TOK + 3].astype(jnp.float32), axis=(0, 2, 3))
    inv_all = lax.rsqrt(total / D + norm_eps)
    inv_scale = inv_all[0][:, None]
    gain_quarter = lax.dynamic_slice_in_dim(norm_gain, mine * QUARTER, QUARTER).reshape(2, 1, HD)
    normal = rows.astype(jnp.float32) * inv_all.reshape(1, 4 * TOK, 1)
    normed = (normal * gain_quarter).astype(jnp.bfloat16)

    products = jnp.einsum(
        "ktc,kbcf->kbtf",
        kv,
        weights,
        preferred_element_type=jnp.float32,
    ).astype(jnp.bfloat16)
    norm_grad = jnp.sum(products.astype(jnp.float32), axis=0)
    gain_part = jnp.sum(norm_grad * normal, axis=1)

    sums = jnp.einsum("ktc,btf->kbcf", kv, normed, preferred_element_type=jnp.float32)
    first = lax.axis_index("zh") == 0
    given = jnp.where(first, sums[:, 1], sums[:, 0]).astype(jnp.bfloat16).reshape(8 * HD, HD)
    terms = terms_of(gain_part).reshape(6, HD)
    came = swap(jnp.concatenate([given, jnp.pad(terms, ((0, 10), (0, 0)))]), "zh", 1)
    kept = jnp.where(first, sums[:, 0], sums[:, 1])
    kept = kept + came[: 8 * HD].astype(jnp.float32).reshape(8, HD, HD)
    gain_part = whole_of(terms) + whole_of(came[8 * HD : 8 * HD + 6])

    back = norm_grad.astype(jnp.bfloat16)
    near = swap(back[:, 2 * TOK :].reshape(4 * TOK, HD), "x", 3)
    near, kept, gain_part = lax.optimization_barrier((near, kept, gain_part))
    near = near.reshape(2, 2 * TOK, HD)

    gain_rows = jnp.pad(terms_of(gain_part).reshape(6, HD), ((0, 2), (0, 0)))
    gain_rows = jnp.broadcast_to(gain_rows[None], (8, 8, HD))
    pieces = jnp.concatenate([kept.astype(jnp.bfloat16), gain_rows], axis=1)
    arrived = exchange(pieces, "y")

    given = jnp.concatenate([back[:, TOK : 2 * TOK], near[:, TOK:]]).reshape(4 * TOK, HD)
    far = swap(given, "x", 1).reshape(2, 2, TOK, HD)

    full = jnp.zeros((8, TOK, HD), jnp.bfloat16)
    for part, r in ((back[:, :TOK], 0), (far[0], 1), (near[:, :TOK], 3), (far[1], 2)):
        full = lax.dynamic_update_slice_in_dim(full, part, (mine ^ r) * 2, axis=0)
    full = jnp.concatenate([full[i] for i in range(8)], axis=1)
    scaled = full.astype(jnp.float32) * norm_gain[None, :]
    normal = widened * inv_scale
    inner = jnp.sum(scaled * normal, axis=1)
    block = jnp.sum(arrived[:, :HD].astype(jnp.float32), axis=0)
    gains = jnp.sum(arrived[:, HD : HD + 6].astype(jnp.float32), axis=0)
    gains = jnp.sum(gains.reshape(3, 2, HD), axis=0)
    inner, gains, block = lax.optimization_barrier((inner, gains, block))
    weight_grad = lax.ppermute(block, AXES, [(b, a) for a, b in moves])
    inner = inner + swap(inner, "core", 1)
    both = jnp.concatenate([inner[None], gains])
    both = exchange(jnp.broadcast_to(both[None], (16, 3, HD)), ("x", "zl")).reshape(4, 4, 3, HD)
    both, weight_grad = lax.optimization_barrier((both, weight_grad))
    inner = lax.dynamic_index_in_dim(both[:, :, 0], mine, 0, keepdims=False)
    inner = jnp.sum(inner, axis=0)[:, None] / D
    gains = lax.dynamic_index_in_dim(both[:, :, 1:], lax.axis_index("zl"), 1, keepdims=False)
    gain_grad = gains.reshape(4 * QUARTER)
    input_grad = (
        residual_grad.astype(jnp.float32) + inv_scale * (scaled - normal * inner)
    ).astype(jnp.bfloat16)
    return (input_grad, weight_grad, gain_grad)


def solution(mesh):
    fine = Mesh(mesh.devices.reshape(SIZES), AXES)
    return jax.shard_map(
        shards,
        mesh=fine,
        in_specs=(
            P(DP, TENSOR),
            P(DP, TENSOR),
            P(DP, TENSOR),
            P(TENSOR, DP),
            P(TENSOR),
        ),
        out_specs=(P(DP, TENSOR), P(TENSOR, DP), P(TENSOR)),
        check_vma=False,
    )
```

```python
import jax
import jax.numpy as jnp
from jax import lax
from jax.sharding import Mesh
from jax.sharding import PartitionSpec as P

D = 8192
HD = 128
TOK = 128
QUARTER = 256

rope_theta = 500000.0
norm_eps = 1e-05

SIZES = (4, 8, 2, 4, 2)
AXES = ("x", "y", "zh", "zl", "core")
DP = ("x", "y", "zh")
TENSOR = ("zl", "core")
ROW = ("y", "zh")


def flat_index(x, y, zh, zl, core):
    return (((x * 8 + y) * 2 + zh) * 4 + zl) * 2 + core


def weight_moves():
    moves = []
    for x in range(4):
        for y in range(8):
            for zh in range(2):
                for zl in range(4):
                    for core in range(2):
                        far_zl, far_core = x, y // 4
                        place = (far_zl ^ zl) * 2 + (far_core ^ core)
                        there = flat_index(y % 4, place, zh, far_zl, far_core)
                        moves.append((flat_index(x, y, zh, zl, core), there))
    return moves


def exchange(value, axes):
    return lax.all_to_all(value, axes, split_axis=0, concat_axis=0, tiled=True)


def swap(value, axis, mask):
    count = lax.axis_size(axis)
    return lax.ppermute(value, axis, [(i, i ^ mask) for i in range(count)])


def terms_of(value):
    first = lax.reduce_precision(value, 8, 7)
    second = lax.reduce_precision(value - first, 8, 7)
    third = value - first - second
    return jnp.stack([first, second, third]).astype(jnp.bfloat16)


def rope_tables(positions_count, head_size):
    half_head = head_size // 2
    frequency = rope_theta ** (-(jnp.arange(half_head, dtype=jnp.float32) * 2.0 / head_size))
    angles = jnp.arange(positions_count, dtype=jnp.float32)[:, None] * frequency[None, :]
    return (jnp.cos(angles), jnp.sin(angles))


def shards(layer_input, residual_grad, key_value_grad, kv_weight, norm_gain):
    moves = weight_moves()
    mine = lax.axis_index("x")

    cosine, sine = rope_tables(TOK, HD)
    grads = key_value_grad.astype(jnp.float32)
    low, high = grads[:, : HD // 2], grads[:, HD // 2 :]
    turned = jnp.concatenate([low * cosine + high * sine, high * cosine - low * sine], axis=1)
    kv_pre = jnp.where(lax.axis_index("core") == 0, turned, grads).astype(jnp.bfloat16)
    widened = layer_input.astype(jnp.float32)
    squares = terms_of(jnp.sum(widened * widened, axis=1))
    packet = jnp.concatenate([kv_pre, jnp.pad(squares, ((0, 13), (0, 0)))], axis=0)[None]

    blocks = jnp.stack([layer_input[:, i * HD : (i + 1) * HD] for i in range(8)])

    def quarter(r):
        return lax.dynamic_slice_in_dim(blocks, (mine ^ r) * 2, 2, axis=0)

    given = jnp.concatenate([quarter(3), quarter(2)]).reshape(4 * TOK, HD)
    packet, given, kv_weight = lax.optimization_barrier((packet, given, kv_weight))

    moved = lax.ppermute(kv_weight, AXES, moves)
    other = lax.ppermute(kv_weight, AXES, [(a, b ^ 8) for a, b in moves])

    packet = jnp.concatenate([packet, swap(packet, "zl", 1)])
    packet, moved, other = lax.optimization_barrier((packet, moved, other))
    first = lax.axis_index("zh") == 0
    weights = jnp.stack([jnp.where(first, moved, other), jnp.where(first, other, moved)])
    for mask, place in ((4, 0), (2, 1), (1, 2)):
        other = swap(weights, "y", mask)
        first = (lax.axis_index("y") & mask) == 0
        pair = [jnp.where(first, weights, other), jnp.where(first, other, weights)]
        weights = jnp.stack(pair, axis=place)
    weights = weights.reshape(8, 2, HD, HD)
    near = swap(given, "x", 3)
    packet = jnp.concatenate([packet, swap(packet, "zl", 2)])
    packet, near = lax.optimization_barrier((packet, near))

    near = near.reshape(2, 2, TOK, HD)
    given = jnp.concatenate([quarter(1), near[1]]).reshape(4 * TOK, HD)
    came = swap(jnp.concatenate([packet.reshape(4 * (TOK + 16), HD), given]), "x", 1)
    far = came[4 * (TOK + 16) :].reshape(2, 2, TOK, HD)
    rows = jnp.concatenate([quarter(0), far[0], near[0], far[1]], axis=1)
    packet = jnp.stack([packet, came[: 4 * (TOK + 16)].reshape(4, TOK + 16, HD)])
    packet = jnp.concatenate([packet, swap(packet, "x", 3)])
    packet = jnp.stack([packet, swap(packet, "core", 1)])

    kv = packet[:, :, :, :TOK].transpose(2, 0, 1, 3, 4).reshape(8, 4 * TOK, HD)
    total = jnp.sum(packet[:, :, :, TOK : TOK + 3].astype(jnp.float32), axis=(0, 2, 3))
    inv_all = lax.rsqrt(total / D + norm_eps)
    inv_scale = inv_all[0][:, None]
    gain_quarter = lax.dynamic_slice_in_dim(norm_gain, mine * QUARTER, QUARTER).reshape(2, 1, HD)
    normal = rows.astype(jnp.float32) * inv_all.reshape(1, 4 * TOK, 1)
    normed = (normal * gain_quarter).astype(jnp.bfloat16)

    products = jnp.einsum(
        "ktc,kbcf->kbtf",
        kv,
        weights,
        preferred_element_type=jnp.float32,
    ).astype(jnp.bfloat16)
    norm_grad = jnp.sum(products.astype(jnp.float32), axis=0)
    gain_part = terms_of(jnp.sum(norm_grad * normal, axis=1)).reshape(6, HD)

    pieces = jnp.einsum(
        "ktc,btf->kbcf", kv, normed, preferred_element_type=jnp.float32
    ).astype(jnp.bfloat16)
    gain_rows = jnp.broadcast_to(jnp.pad(gain_part, ((0, 2), (0, 0)))[None], (16, 8, HD))
    arrived = exchange(jnp.concatenate([pieces.reshape(16, HD, HD), gain_rows], axis=1), ROW)
    block = jnp.sum(arrived[:, :HD].astype(jnp.float32), axis=0)
    weight_grad = lax.ppermute(block, AXES, [(b, a) for a, b in moves])
    gains = jnp.sum(arrived[:, HD : HD + 6].astype(jnp.float32), axis=0)
    gains = jnp.sum(gains.reshape(3, 2, HD), axis=0)
    gains = exchange(jnp.broadcast_to(gains[None], (4, 2, HD)), "x")
    gain_grad = gains.reshape(4 * QUARTER)

    back = norm_grad.astype(jnp.bfloat16)
    near = swap(back[:, 2 * TOK :].reshape(4 * TOK, HD), "x", 3).reshape(2, 2 * TOK, HD)
    given = jnp.concatenate([back[:, TOK : 2 * TOK], near[:, TOK:]]).reshape(4 * TOK, HD)
    far = swap(given, "x", 1).reshape(2, 2, TOK, HD)

    full = jnp.zeros((8, TOK, HD), jnp.bfloat16)
    for part, r in ((back[:, :TOK], 0), (far[0], 1), (near[:, :TOK], 3), (far[1], 2)):
        full = lax.dynamic_update_slice_in_dim(full, part, (mine ^ r) * 2, axis=0)
    full = jnp.concatenate([full[i] for i in range(8)], axis=1)
    scaled = full.astype(jnp.float32) * norm_gain[None, :]
    normal = widened * inv_scale
    inner = jnp.sum(scaled * normal, axis=1)
    for axis, mask in (("core", 1), ("zl", 1), ("zl", 2)):
        inner = inner + swap(inner, axis, mask)
    inner = inner[:, None] / D
    input_grad = (
        residual_grad.astype(jnp.float32) + inv_scale * (scaled - normal * inner)
    ).astype(jnp.bfloat16)
    return (input_grad, weight_grad, gain_grad)


def solution(mesh):
    fine = Mesh(mesh.devices.reshape(SIZES), AXES)
    return jax.shard_map(
        shards,
        mesh=fine,
        in_specs=(
            P(DP, TENSOR),
            P(DP, TENSOR),
            P(DP, TENSOR),
            P(TENSOR, DP),
            P(TENSOR),
        ),
        out_specs=(P(DP, TENSOR), P(TENSOR, DP), P(TENSOR)),
        check_vma=False,
    )
```

```python
import jax
import jax.numpy as jnp
from jax import lax
from jax.sharding import Mesh
from jax.sharding import PartitionSpec as P

D = 8192
HD = 128
TOK = 128
QUARTER = 256

rope_theta = 500000.0
norm_eps = 1e-05

SIZES = (4, 8, 2, 4, 2)
AXES = ("x", "y", "zh", "zl", "core")
DP = ("x", "y", "zh")
TENSOR = ("zl", "core")
ROW = ("y", "zh")


def flat_index(x, y, zh, zl, core):
    return (((x * 8 + y) * 2 + zh) * 4 + zl) * 2 + core


def weight_moves():
    moves = []
    for x in range(4):
        for y in range(8):
            for zh in range(2):
                for zl in range(4):
                    for core in range(2):
                        far_zl, far_core = x, y // 4
                        place = (far_zl ^ zl) * 2 + (far_core ^ core)
                        there = flat_index(y % 4, place, zh, far_zl, far_core)
                        moves.append((flat_index(x, y, zh, zl, core), there))
    return moves


def exchange(value, axes):
    return lax.all_to_all(value, axes, split_axis=0, concat_axis=0, tiled=True)


def swap(value, axis, mask):
    count = lax.axis_size(axis)
    return lax.ppermute(value, axis, [(i, i ^ mask) for i in range(count)])


def terms_of(value):
    first = lax.reduce_precision(value, 8, 7)
    second = lax.reduce_precision(value - first, 8, 7)
    third = value - first - second
    return jnp.stack([first, second, third]).astype(jnp.bfloat16)


def rope_tables(positions_count, head_size):
    half_head = head_size // 2
    frequency = rope_theta ** (-(jnp.arange(half_head, dtype=jnp.float32) * 2.0 / head_size))
    angles = jnp.arange(positions_count, dtype=jnp.float32)[:, None] * frequency[None, :]
    return (jnp.cos(angles), jnp.sin(angles))


def shards(layer_input, residual_grad, key_value_grad, kv_weight, norm_gain):
    moves = weight_moves()
    mine = lax.axis_index("x")

    moved = lax.ppermute(kv_weight, AXES, moves)

    cosine, sine = rope_tables(TOK, HD)
    grads = key_value_grad.astype(jnp.float32)
    low, high = grads[:, : HD // 2], grads[:, HD // 2 :]
    turned = jnp.concatenate([low * cosine + high * sine, high * cosine - low * sine], axis=1)
    kv_pre = jnp.where(lax.axis_index("core") == 0, turned, grads).astype(jnp.bfloat16)
    widened = layer_input.astype(jnp.float32)
    squares = terms_of(jnp.sum(widened * widened, axis=1))
    packet = jnp.concatenate([kv_pre, jnp.pad(squares, ((0, 13), (0, 0)))], axis=0)[None]

    blocks = jnp.stack([layer_input[:, i * HD : (i + 1) * HD] for i in range(8)])

    def quarter(r):
        return lax.dynamic_slice_in_dim(blocks, (mine ^ r) * 2, 2, axis=0)

    packet = jnp.concatenate([packet, swap(packet, "zl", 1)])
    packet, moved = lax.optimization_barrier((packet, moved))
    weights = moved
    for axis, mask, place in (("zh", 1, 0), ("y", 4, 0), ("y", 2, 1), ("y", 1, 2)):
        other = swap(weights, axis, mask)
        first = (lax.axis_index(axis) & mask) == 0
        pair = [jnp.where(first, weights, other), jnp.where(first, other, weights)]
        weights = jnp.stack(pair, axis=place)
    weights = weights.reshape(8, 2, HD, HD)
    given = jnp.concatenate([quarter(3), quarter(2)]).reshape(4 * TOK, HD)
    near = swap(given, "x", 3)
    packet = jnp.concatenate([packet, swap(packet, "zl", 2)])
    packet, near = lax.optimization_barrier((packet, near))

    near = near.reshape(2, 2, TOK, HD)
    given = jnp.concatenate([quarter(1), near[1]]).reshape(4 * TOK, HD)
    came = swap(jnp.concatenate([packet.reshape(4 * (TOK + 16), HD), given]), "x", 1)
    far = came[4 * (TOK + 16) :].reshape(2, 2, TOK, HD)
    rows = jnp.concatenate([quarter(0), far[0], near[0], far[1]], axis=1)
    packet = jnp.stack([packet, came[: 4 * (TOK + 16)].reshape(4, TOK + 16, HD)])
    packet = jnp.concatenate([packet, swap(packet, "x", 3)])
    packet = jnp.stack([packet, swap(packet, "core", 1)])

    kv = packet[:, :, :, :TOK].transpose(2, 0, 1, 3, 4).reshape(8, 4 * TOK, HD)
    total = jnp.sum(packet[:, :, :, TOK : TOK + 3].astype(jnp.float32), axis=(0, 2, 3))
    inv_all = lax.rsqrt(total / D + norm_eps)
    inv_scale = inv_all[0][:, None]
    gain_quarter = lax.dynamic_slice_in_dim(norm_gain, mine * QUARTER, QUARTER).reshape(2, 1, HD)
    normal = rows.astype(jnp.float32) * inv_all.reshape(1, 4 * TOK, 1)
    normed = (normal * gain_quarter).astype(jnp.bfloat16)

    products = jnp.einsum(
        "ktc,kbcf->kbtf",
        kv,
        weights,
        preferred_element_type=jnp.float32,
    ).astype(jnp.bfloat16)
    norm_grad = jnp.sum(products.astype(jnp.float32), axis=0)
    gain_part = terms_of(jnp.sum(norm_grad * normal, axis=1)).reshape(6, HD)

    pieces = jnp.einsum(
        "ktc,btf->kbcf", kv, normed, preferred_element_type=jnp.float32
    ).astype(jnp.bfloat16)
    gain_rows = jnp.broadcast_to(jnp.pad(gain_part, ((0, 2), (0, 0)))[None], (16, 8, HD))
    arrived = exchange(jnp.concatenate([pieces.reshape(16, HD, HD), gain_rows], axis=1), ROW)
    block = jnp.sum(arrived[:, :HD].astype(jnp.float32), axis=0)
    weight_grad = lax.ppermute(block, AXES, [(b, a) for a, b in moves])
    gains = jnp.sum(arrived[:, HD : HD + 6].astype(jnp.float32), axis=0)
    gains = jnp.sum(gains.reshape(3, 2, HD), axis=0)
    gains = exchange(jnp.broadcast_to(gains[None], (4, 2, HD)), "x")
    gain_grad = gains.reshape(4 * QUARTER)

    back = norm_grad.astype(jnp.bfloat16)
    near = swap(back[:, 2 * TOK :].reshape(4 * TOK, HD), "x", 3).reshape(2, 2 * TOK, HD)
    given = jnp.concatenate([back[:, TOK : 2 * TOK], near[:, TOK:]]).reshape(4 * TOK, HD)
    far = swap(given, "x", 1).reshape(2, 2, TOK, HD)

    full = jnp.zeros((8, TOK, HD), jnp.bfloat16)
    for part, r in ((back[:, :TOK], 0), (far[0], 1), (near[:, :TOK], 3), (far[1], 2)):
        full = lax.dynamic_update_slice_in_dim(full, part, (mine ^ r) * 2, axis=0)
    full = jnp.concatenate([full[i] for i in range(8)], axis=1)
    scaled = full.astype(jnp.float32) * norm_gain[None, :]
    normal = widened * inv_scale
    inner = jnp.sum(scaled * normal, axis=1)
    for axis, mask in (("core", 1), ("zl", 1), ("zl", 2)):
        inner = inner + swap(inner, axis, mask)
    inner = inner[:, None] / D
    input_grad = (
        residual_grad.astype(jnp.float32) + inv_scale * (scaled - normal * inner)
    ).astype(jnp.bfloat16)
    return (input_grad, weight_grad, gain_grad)


def solution(mesh):
    fine = Mesh(mesh.devices.reshape(SIZES), AXES)
    return jax.shard_map(
        shards,
        mesh=fine,
        in_specs=(
            P(DP, TENSOR),
            P(DP, TENSOR),
            P(DP, TENSOR),
            P(TENSOR, DP),
            P(TENSOR),
        ),
        out_specs=(P(DP, TENSOR), P(TENSOR, DP), P(TENSOR)),
        check_vma=False,
    )
```

```python
import jax
import jax.numpy as jnp
from jax import lax
from jax.sharding import Mesh
from jax.sharding import PartitionSpec as P

D = 8192
HD = 128
TOK = 128
QUARTER = 256

rope_theta = 500000.0
norm_eps = 1e-05

SIZES = (4, 8, 2, 4, 2)
AXES = ("x", "y", "zh", "zl", "core")
DP = ("x", "y", "zh")
TENSOR = ("zl", "core")
ROW = ("y", "zh")


def flat_index(x, y, zh, zl, core):
    return (((x * 8 + y) * 2 + zh) * 4 + zl) * 2 + core


def weight_moves():
    moves = []
    for x in range(4):
        for y in range(8):
            for zh in range(2):
                for zl in range(4):
                    for core in range(2):
                        far_zl, far_core = x, y // 4
                        place = (far_zl ^ zl) * 2 + (far_core ^ core)
                        there = flat_index(y % 4, place, zh, far_zl, far_core)
                        moves.append((flat_index(x, y, zh, zl, core), there))
    return moves


def exchange(value, axes):
    return lax.all_to_all(value, axes, split_axis=0, concat_axis=0, tiled=True)


def swap(value, axis, mask):
    count = lax.axis_size(axis)
    return lax.ppermute(value, axis, [(i, i ^ mask) for i in range(count)])


def terms_of(value):
    first = lax.reduce_precision(value, 8, 7)
    second = lax.reduce_precision(value - first, 8, 7)
    third = value - first - second
    return jnp.stack([first, second, third]).astype(jnp.bfloat16)


def rope_tables(positions_count, head_size):
    half_head = head_size // 2
    frequency = rope_theta ** (-(jnp.arange(half_head, dtype=jnp.float32) * 2.0 / head_size))
    angles = jnp.arange(positions_count, dtype=jnp.float32)[:, None] * frequency[None, :]
    return (jnp.cos(angles), jnp.sin(angles))


def shards(layer_input, residual_grad, key_value_grad, kv_weight, norm_gain):
    moves = weight_moves()
    mine = lax.axis_index("x")

    moved = lax.ppermute(kv_weight, AXES, moves)
    other = lax.ppermute(kv_weight, AXES, [(a, b ^ 8) for a, b in moves])

    cosine, sine = rope_tables(TOK, HD)
    grads = key_value_grad.astype(jnp.float32)
    low, high = grads[:, : HD // 2], grads[:, HD // 2 :]
    turned = jnp.concatenate([low * cosine + high * sine, high * cosine - low * sine], axis=1)
    kv_pre = jnp.where(lax.axis_index("core") == 0, turned, grads).astype(jnp.bfloat16)
    widened = layer_input.astype(jnp.float32)
    squares = terms_of(jnp.sum(widened * widened, axis=1))
    packet = jnp.concatenate([kv_pre, jnp.pad(squares, ((0, 13), (0, 0)))], axis=0)[None]

    blocks = jnp.stack([layer_input[:, i * HD : (i + 1) * HD] for i in range(8)])

    def quarter(r):
        return lax.dynamic_slice_in_dim(blocks, (mine ^ r) * 2, 2, axis=0)

    packet = jnp.concatenate([packet, swap(packet, "zl", 1)])
    packet, moved, other = lax.optimization_barrier((packet, moved, other))
    first = lax.axis_index("zh") == 0
    weights = jnp.stack([jnp.where(first, moved, other), jnp.where(first, other, moved)])
    for mask, place in ((4, 0), (2, 1), (1, 2)):
        other = swap(weights, "y", mask)
        first = (lax.axis_index("y") & mask) == 0
        pair = [jnp.where(first, weights, other), jnp.where(first, other, weights)]
        weights = jnp.stack(pair, axis=place)
    weights = weights.reshape(8, 2, HD, HD)
    given = jnp.concatenate([quarter(3), quarter(2)]).reshape(4 * TOK, HD)
    near = swap(given, "x", 3)
    packet = jnp.concatenate([packet, swap(packet, "zl", 2)])
    packet, near = lax.optimization_barrier((packet, near))

    near = near.reshape(2, 2, TOK, HD)
    given = jnp.concatenate([quarter(1), near[1]]).reshape(4 * TOK, HD)
    came = swap(jnp.concatenate([packet.reshape(4 * (TOK + 16), HD), given]), "x", 1)
    far = came[4 * (TOK + 16) :].reshape(2, 2, TOK, HD)
    rows = jnp.concatenate([quarter(0), far[0], near[0], far[1]], axis=1)
    packet = jnp.stack([packet, came[: 4 * (TOK + 16)].reshape(4, TOK + 16, HD)])
    packet = jnp.concatenate([packet, swap(packet, "x", 3)])
    packet = jnp.stack([packet, swap(packet, "core", 1)])

    kv = packet[:, :, :, :TOK].transpose(2, 0, 1, 3, 4).reshape(8, 4 * TOK, HD)
    total = jnp.sum(packet[:, :, :, TOK : TOK + 3].astype(jnp.float32), axis=(0, 2, 3))
    inv_all = lax.rsqrt(total / D + norm_eps)
    inv_scale = inv_all[0][:, None]
    gain_quarter = lax.dynamic_slice_in_dim(norm_gain, mine * QUARTER, QUARTER).reshape(2, 1, HD)
    normal = rows.astype(jnp.float32) * inv_all.reshape(1, 4 * TOK, 1)
    normed = (normal * gain_quarter).astype(jnp.bfloat16)

    products = jnp.einsum(
        "ktc,kbcf->kbtf",
        kv,
        weights,
        preferred_element_type=jnp.float32,
    ).astype(jnp.bfloat16)
    norm_grad = jnp.sum(products.astype(jnp.float32), axis=0)
    gain_part = terms_of(jnp.sum(norm_grad * normal, axis=1)).reshape(6, HD)

    pieces = jnp.einsum(
        "ktc,btf->kbcf", kv, normed, preferred_element_type=jnp.float32
    ).astype(jnp.bfloat16)
    gain_rows = jnp.broadcast_to(jnp.pad(gain_part, ((0, 2), (0, 0)))[None], (16, 8, HD))
    arrived = exchange(jnp.concatenate([pieces.reshape(16, HD, HD), gain_rows], axis=1), ROW)
    block = jnp.sum(arrived[:, :HD].astype(jnp.float32), axis=0)
    weight_grad = lax.ppermute(block, AXES, [(b, a) for a, b in moves])
    gains = jnp.sum(arrived[:, HD : HD + 6].astype(jnp.float32), axis=0)
    gains = jnp.sum(gains.reshape(3, 2, HD), axis=0)
    gains = exchange(jnp.broadcast_to(gains[None], (4, 2, HD)), "x")
    gain_grad = gains.reshape(4 * QUARTER)

    back = norm_grad.astype(jnp.bfloat16)
    near = swap(back[:, 2 * TOK :].reshape(4 * TOK, HD), "x", 3).reshape(2, 2 * TOK, HD)
    given = jnp.concatenate([back[:, TOK : 2 * TOK], near[:, TOK:]]).reshape(4 * TOK, HD)
    far = swap(given, "x", 1).reshape(2, 2, TOK, HD)

    full = jnp.zeros((8, TOK, HD), jnp.bfloat16)
    for part, r in ((back[:, :TOK], 0), (far[0], 1), (near[:, :TOK], 3), (far[1], 2)):
        full = lax.dynamic_update_slice_in_dim(full, part, (mine ^ r) * 2, axis=0)
    full = jnp.concatenate([full[i] for i in range(8)], axis=1)
    scaled = full.astype(jnp.float32) * norm_gain[None, :]
    normal = widened * inv_scale
    inner = jnp.sum(scaled * normal, axis=1)
    inner = inner + swap(inner, "core", 1)
    inner = inner + swap(inner, "zl", 1) + swap(inner, "zl", 2) + swap(inner, "zl", 3)
    inner = inner[:, None] / D
    input_grad = (
        residual_grad.astype(jnp.float32) + inv_scale * (scaled - normal * inner)
    ).astype(jnp.bfloat16)
    return (input_grad, weight_grad, gain_grad)


def solution(mesh):
    fine = Mesh(mesh.devices.reshape(SIZES), AXES)
    return jax.shard_map(
        shards,
        mesh=fine,
        in_specs=(
            P(DP, TENSOR),
            P(DP, TENSOR),
            P(DP, TENSOR),
            P(TENSOR, DP),
            P(TENSOR),
        ),
        out_specs=(P(DP, TENSOR), P(TENSOR, DP), P(TENSOR)),
        check_vma=False,
    )
```
